256 devices in a mesh: seq: 64 (over z, x, core), mp: 4 (over y).
Axes of the slice: x: 4, y: 4, z: 8, core: 2. Of those that a mesh axis runs over, the one named last changes fastest.
Arguments:
- tiles: bfloat16 [32768, 768], P('seq'), may hold values from -6 to 6
- w_qkv: bfloat16 [768, 2304], P(None, 'mp'), may hold values from -0.3125 to 0.3125
- w_out: bfloat16 [768, 768], P('mp'), may hold values from -0.4375 to 0.4375
- slide_lengths: int32 [4], replicated, may hold values from 1 to 16384, 32768 in all
- drop_salt: int32 [1], replicated, may hold values from 0 to 1048575
- cotangent: bfloat16 [32768, 768], P('seq'), may hold values from -6 to 6
Outputs:
- layer_out: bfloat16 [32768, 768], P('seq')
- tile_gradient: bfloat16 [32768, 768], P('seq')
- grad_w_qkv: float32 [768, 2304], P(None, 'mp')
- grad_w_out: float32 [768, 768], P('mp')
The draws below stay inside these ranges and needn't reach their ends.
Inputs may be any that keep to these rules, and one draw needn't show every extreme that they name: `slide_lengths`: the four lengths sum to 32768; the longest slide holds exactly 16384 tiles.
All inputs are finite; a program needn't handle non-finite values.
Results may differ from the reference program's by a relative error of at most 0.017.
Values may be sent and summed in bfloat16 or wider, within the bound.
No kernel may reach another device: no remote copies, remote signals or barrier semaphores. Data moves between devices by JAX's collectives and lax.ppermute only.
A program may use at most 128 MiB of HBM per device.

```python
import math
import jax
import jax.numpy as jnp
import numpy as np
from jax import lax

D = 768
HD = 48
TOK_DEV = 512
SEG_LOCAL = 512
G_NEAR = 4
G_MID = 16
TOKENS = 32768
N_SEQ = 64


def level_of(own_key, shape, split, smallest, high):
    def one(position, shards_of):
        draws = jax.random.uniform(jax.random.fold_in(jax.random.fold_in(own_key, 6), position), (shards_of,), jnp.float32, smallest / len(split), high / len(split))
        return jnp.repeat(jnp.exp(draws), shape[position] // shards_of).reshape((-1,) + (1,) * (len(shape) - position - 1))

    gain = one(*split[0])
    for cut in split[1:]:
        gain = gain * one(*cut)
    return gain


def length_profile(count, total, most, lean):
    portions = [(1 << 20) // math.isqrt(grade ** lean) + 1 for grade in range(2, count + 1)]
    rest, given = total - most - (count - 1), [1] * (count - 1)
    while rest > 0:
        free = [i for i in range(count - 1) if given[i] < most]
        mass, left = sum([portions[i] for i in free]), rest
        for i in free:
            addition = min(most - given[i], max(1, left * portions[i] // mass), rest)
            given[i] = given[i] + addition
            rest = rest - addition
    return np.array([most] + given)


def uneven_parts(stream_key, number_of, total, reach, slope):
    if number_of == 2:
        one = jax.random.randint(stream_key, (), max(1, total - reach), min(reach, total - 1) + 1)
        return jnp.stack([one, total - one])
    tallies = jnp.asarray(length_profile(number_of, total, reach, slope), jnp.int32)
    couples = (number_of - 1) // 2
    giver, receiver = tallies[1:1 + 2 * couples:2], tallies[2:2 + 2 * couples:2]
    room = jnp.minimum(giver - 1, reach - receiver)
    shifted = jax.random.randint(jax.random.fold_in(stream_key, 1), (couples,), 0, 1 << 20) % (room + 1)
    tallies = tallies.at[1:1 + 2 * couples:2].set(giver - shifted).at[2:2 + 2 * couples:2].set(receiver + shifted)
    return tallies[jax.random.permutation(jax.random.fold_in(stream_key, 2), number_of)]


def bell_draw(own_key, shape, scale, limit, split=(), kind=jnp.bfloat16):
    entries = scale * jax.random.normal(own_key, shape, jnp.float32)
    if split:
        entries = entries * level_of(own_key, shape, split, -0.22, 0.18)
    return jnp.clip(entries, -limit, limit).astype(kind)


def setup_inputs(seed: int = 0) -> dict:
    key_of = jax.random.split(jax.random.key(seed), 7)
    tiles = bell_draw(key_of[0], (TOKENS, D), 1.0, 6.0, ((0, 64),))
    w_qkv = bell_draw(key_of[1], (D, 3 * D), (D // 2) ** -0.5, 0.3125, ((1, 4),))
    w_out = bell_draw(key_of[2], (D, D), (D // 4) ** -0.5, 0.4375, ((0, 4),))
    slide_lengths = uneven_parts(key_of[3], 4, TOKENS, TOKENS // 2, 2).astype(jnp.int32)
    drop_salt = jax.random.randint(key_of[4], (1,), 0, 1048576).astype(jnp.int32)
    cotangent = bell_draw(key_of[5], (TOKENS, D), 1.0, 6.0, ((0, 64),))
    return dict(tiles=tiles, w_qkv=w_qkv, w_out=w_out, slide_lengths=slide_lengths, drop_salt=drop_salt, cotangent=cotangent)


drop_scale = 1024.0 / 922.0

def keep_mask(salt, positions, features):
    index = positions * D + features
    mixed = index * 747796405 + salt
    mixed = mixed ^ mixed >> 13
    mixed = mixed * 1274126177
    mixed = mixed ^ mixed >> 16
    return mixed & 1023 >= 102

def slide_of(positions, slide_lengths):
    ends = jnp.cumsum(slide_lengths).astype(jnp.int32)
    return lax.optimization_barrier(jnp.sum((positions[..., None] >= ends[:3]).astype(jnp.int32), -1))

def weights_of(queries, keys_in, slide_ids):
    factor = HD ** (-0.5)
    scores = jnp.einsum('qd,kd->qk', queries.astype(jnp.float32), keys_in.astype(jnp.float32)) * factor
    allowed = slide_ids[:, None] == slide_ids[None, :]
    return jnp.exp(jnp.where(allowed, scores, -1e+30))

def stats_pass(pieces):
    queries, keys_in, values_in, slide_ids = pieces
    weights = weights_of(queries, keys_in, slide_ids)
    return (lax.optimization_barrier(jnp.sum(weights, -1)), jnp.einsum('qk,kd->qd', weights, values_in.astype(jnp.float32)))

def grad_pass(pieces):
    queries, keys_in, values_in, grad_out, slide_ids, total, delta = pieces
    factor = HD ** (-0.5)
    query_wide = queries.astype(jnp.float32)
    key_wide = keys_in.astype(jnp.float32)
    value_wide = values_in.astype(jnp.float32)
    grad_wide = grad_out.astype(jnp.float32)
    weights = weights_of(queries, keys_in, slide_ids)
    shares = weights / total[:, None]
    shares_low = shares.astype(jnp.bfloat16).astype(jnp.float32)
    outputs = jnp.einsum('qk,kd->qd', shares_low, value_wide)
    grad_values = jnp.einsum('qk,qd->kd', shares_low, grad_wide)
    grad_shares = jnp.einsum('qd,kd->qk', grad_wide, value_wide)
    centred = grad_shares - delta[:, None]
    grad_scores = (shares * centred).astype(jnp.bfloat16).astype(jnp.float32)
    grad_queries = jnp.einsum('qk,kd->qd', grad_scores, key_wide) * factor
    grad_keys = jnp.einsum('qk,qd->kd', grad_scores, query_wide) * factor
    return (outputs, grad_queries, grad_keys, grad_values)

def pick(array, rate, offset, segment):
    chosen = array.reshape((TOKENS // rate, rate) + array.shape[1:])[:, offset]
    return chosen.reshape((TOKENS // segment, segment // rate) + array.shape[1:])

def spread(selected, rate, offset):
    holder = jnp.zeros((selected.shape[0], rate) + selected.shape[1:], selected.dtype)
    return holder.at[:, offset].set(selected).reshape((selected.shape[0] * rate,) + selected.shape[1:])

def reference(tiles, w_qkv, w_out, slide_lengths, drop_salt, cotangent):
    wide = tiles.astype(jnp.float32)
    centered_input = wide - lax.optimization_barrier(jnp.mean(wide, -1, keepdims=True))
    inverse_deviation = lax.rsqrt(lax.optimization_barrier(jnp.mean(centered_input * centered_input, -1, keepdims=True)) + 1e-05)
    standardized_input = centered_input * inverse_deviation
    normalized_rows = standardized_input.astype(jnp.bfloat16)
    qkv = jnp.dot(normalized_rows, w_qkv, preferred_element_type=jnp.float32).astype(jnp.bfloat16)
    qkv = qkv.reshape(TOKENS, 4, 3, 4, HD)
    positions = jnp.arange(TOKENS, dtype=jnp.int32)
    slide = slide_of(positions, slide_lengths)
    keeper = keep_mask(drop_salt[0], positions[:, None], jnp.arange(D, dtype=jnp.int32)[None, :])
    drop_factor = jnp.where(keeper, drop_scale, 0.0).astype(jnp.float32)
    grad_branch = (cotangent.astype(jnp.float32) * drop_factor).astype(jnp.bfloat16)
    grad_heads = jnp.dot(grad_branch, w_out.T, preferred_element_type=jnp.float32).astype(jnp.bfloat16)
    grad_heads = grad_heads.reshape(TOKENS, 4, 4, HD)
    segments = (SEG_LOCAL, G_NEAR * TOK_DEV, G_MID * TOK_DEV, TOKENS)
    rates = (1, G_NEAR, G_MID, N_SEQ)
    head_outs = []
    head_grads = []
    for head_index in range(16):
        member = head_index // 4
        within = head_index % 4
        parts = (qkv[:, member, 0, within], qkv[:, member, 1, within], qkv[:, member, 2, within])
        grad_out = grad_heads[:, member, within]
        total = jnp.zeros((TOKENS,), jnp.float32)
        numer = jnp.zeros((TOKENS, HD), jnp.float32)
        for config in range(4):
            rate = rates[config]
            segment = segments[config]
            offset = head_index % rate
            picks = tuple((pick(array, rate, offset, segment) for array in parts))
            picks = picks + (pick(slide, rate, offset, segment),)
            sums, partial_sum = lax.map(stats_pass, picks)
            total = total + spread(sums.reshape(TOKENS // rate), rate, offset)
            numer = numer + spread(partial_sum.reshape(TOKENS // rate, HD), rate, offset)
        mixed = numer / total[:, None]
        delta = lax.optimization_barrier(jnp.sum(grad_out.astype(jnp.float32) * mixed, -1))
        sums_out = [jnp.zeros((TOKENS, HD), jnp.float32) for which in range(4)]
        for config in range(4):
            rate = rates[config]
            segment = segments[config]
            offset = head_index % rate
            picks = tuple((pick(array, rate, offset, segment) for array in parts + (grad_out, slide, total, delta)))
            results = lax.map(grad_pass, picks)
            for which in range(4):
                sums_out[which] = sums_out[which] + spread(results[which].reshape(TOKENS // rate, HD), rate, offset)
        head_outs.append(sums_out[0].astype(jnp.bfloat16))
        head_grads.append(tuple((entry.astype(jnp.bfloat16) for entry in sums_out[1:])))
    heads_out = jnp.stack(head_outs, 1).reshape(TOKENS, D)
    grad_qkv = jnp.stack([jnp.stack([jnp.stack([head_grads[4 * member + within][which] for within in range(4)], 1) for which in range(3)], 1) for member in range(4)], 1)
    grad_qkv = grad_qkv.reshape(TOKENS, 3 * D)
    quarter = D // 4
    proj = jnp.zeros((TOKENS, D), jnp.float32)
    normalized_gradient = jnp.zeros((TOKENS, D), jnp.float32)
    for member in range(4):
        term = jnp.dot(heads_out[:, member * quarter:(member + 1) * quarter], w_out[member * quarter:(member + 1) * quarter], preferred_element_type=jnp.float32)
        proj = proj + term.astype(jnp.bfloat16).astype(jnp.float32)
        back = jnp.dot(grad_qkv[:, member * 3 * quarter:(member + 1) * 3 * quarter], w_qkv[:, member * 3 * quarter:(member + 1) * 3 * quarter].T, preferred_element_type=jnp.float32)
        normalized_gradient = normalized_gradient + back.astype(jnp.bfloat16).astype(jnp.float32)
    layer_out = (proj * drop_factor).astype(jnp.bfloat16)
    inv_rows = TOKENS ** (-0.5)
    grad_w_out = jnp.dot(heads_out.T, grad_branch, preferred_element_type=jnp.float32) * inv_rows
    grad_w_qkv = jnp.dot(normalized_rows.T, grad_qkv, preferred_element_type=jnp.float32) * inv_rows
    gradient_mean = lax.optimization_barrier(jnp.mean(normalized_gradient, -1, keepdims=True))
    mixed_product_mean = lax.optimization_barrier(jnp.mean(normalized_gradient * standardized_input, -1, keepdims=True))
    tile_gradient = (inverse_deviation * (normalized_gradient - gradient_mean - standardized_input * mixed_product_mean)).astype(jnp.bfloat16)
    return (layer_out, tile_gradient, grad_w_qkv, grad_w_out)
```

```python
import jax
import jax.numpy as jnp
from jax import lax
from jax.experimental import pallas as pl
from jax.experimental.pallas import tpu as pltpu
from jax.sharding import PartitionSpec as P

BF = jnp.bfloat16
F32 = jnp.float32
I32 = jnp.int32
T = 512
D = 768
HD = 48
C = 4 * HD
DROP = 1024.0 / 922.0
FACTOR = HD**-0.5
C1 = FACTOR * 1.4426950408889634
NEG = -1e30


def nt(a, b):
    return lax.dot_general(a, b, (((1,), (1,)), ((), ())), preferred_element_type=F32)


def nn(a, b):
    return lax.dot_general(a, b, (((1,), (0,)), ((), ())), preferred_element_type=F32)


def rows(n, m=1):
    return lax.broadcasted_iota(I32, (n, m), 0)


def lanes(m, n=1):
    return lax.broadcasted_iota(I32, (n, m), 1)


def head_of(x, top):
    total = jnp.zeros_like(x)
    for j in range(1, top):
        total = total + (x >= j * HD).astype(I32)
    return total


def lane_mask(c):
    col = lanes(C)
    return jnp.where((col >= c * HD) & (col < (c + 1) * HD), 1.0, 0.0)


def slide(pos, len_ref):
    e0 = len_ref[0]
    e1 = e0 + len_ref[1]
    e2 = e1 + len_ref[2]
    return (pos >= e0).astype(I32) + (pos >= e1).astype(I32) + (pos >= e2).astype(I32)


def bias_of(a, b):
    return jnp.where(a == b, 0.0, NEG)


def keep(salt, first, n):
    index = (first + rows(n, D)) * D + lanes(D, n)
    mixed = index * 747796405 + salt
    mixed = mixed ^ (mixed >> 13)
    mixed = mixed * 1274126177
    mixed = mixed ^ (mixed >> 16)
    return (mixed & 1023) >= 102


def standard(x):
    wide = x.astype(F32)
    centred = wide - jnp.mean(wide, -1, keepdims=True)
    inv = lax.rsqrt(jnp.mean(centred * centred, -1, keepdims=True) + 1e-05)
    return centred * inv, inv


def off_near(s):
    return ((s & 1) << 1) | (s >> 1)


def off_mid(s):
    return ((s & 1) << 3) | (s & 6) | (s >> 3)


def off_far(s):
    return ((s & 1) << 5) | ((s & 2) << 3) | ((s & 4) << 1) | ((s >> 2) & 6) | (s >> 5)


def base_near(r, place):
    return (place ^ off_near(r >> 7)) * T + (r & 127) * 4


def base_mid(r, place):
    return (place ^ off_mid(r >> 5)) * T + (r & 31) * 16


def base_far(r, place):
    return (place ^ off_far(r >> 3)) * T + (r & 7) * 64


def route_near():
    return jnp.where((lanes(T, 128) >> 2) == rows(128, T), 1.0, 0.0).astype(BF)


def route_mid():
    return jnp.where((lanes(T, 128) >> 4) == (rows(128, T) & 31), 1.0, 0.0).astype(BF)


def route_far():
    r = rows(128, T)
    return jnp.where(((lanes(T, 128) >> 6) == (r & 7)) & (r < 32), 1.0, 0.0).astype(BF)


def spread(a, route, ok):
    half = a * 0.5
    hi = half.astype(BF)
    lo = (half - hi.astype(F32)).astype(BF)
    out = (nn(hi, route) + nn(lo, route)) * 2.0
    return jnp.where(ok, out, 0.0)


def row_head(n):
    r = rows(n)
    h = head_of(jnp.minimum(r, C - 1), 4)
    return jnp.where(r < C, h, (r - C) >> 3)


def turned(x):
    return jnp.transpose(x.astype(F32)).astype(BF)


def branch_kernel(idx, salt, cot, branch):
    drop = jnp.where(keep(salt[0], idx[0] * T, T), DROP, 0.0)
    branch[...] = (cot[...].astype(F32) * drop).astype(BF)


def start_kernel(idx, tiles, w, w_out, branch, x_ref, near, mid, far, normed_ref):
    member = idx[1]
    xhat, _ = standard(tiles[...])
    normed = xhat.astype(BF)
    normed_ref[...] = normed
    x_ref[:, : 3 * C] = nt(normed, w[...]).astype(BF)
    x_ref[:, 3 * C :] = nt(branch[...], w_out[...]).astype(BF)
    x = x_ref[...].astype(F32)
    lane_head = head_of(lanes(D), 16) & 3
    p = rows(T)
    for out, count, rate, shift in ((near, 128, 4, 2), (mid, 32, 16, 4), (far, 8, 64, 6)):
        first = (4 * member) & (rate - 1)
        chosen = jnp.where((p & (rate - 1)) == first + lane_head, x, 0.0).astype(BF)
        n = max(count, 16)
        pick = jnp.where((lanes(T, n) >> shift) == rows(n, T), 1.0, 0.0).astype(BF)
        out[...] = nn(pick, chosen)[:count].astype(BF)


def local_stats_kernel(idx, lens, x_ref, st, vt, bias):
    place = idx[0]
    first = place * T
    q = x_ref[:, :C]
    k = x_ref[:, C : 2 * C]
    vt[...] = turned(x_ref[:, 2 * C : 3 * C])
    bias[...] = bias_of(slide(first + rows(T), lens), slide(first + lanes(T), lens))

    def step(c, carry):
        qc = q * lane_mask(c).astype(BF)
        w = jnp.exp2(nt(k, qc) * C1 + bias[...])
        top = pl.multiple_of(c * HD, 16)
        st[pl.ds(top, HD), :] = nn(vt[pl.ds(top, HD), :], w.astype(BF))
        st[pl.ds(pl.multiple_of(C + 8 * c, 8), 8), :] = jnp.broadcast_to(
            jnp.sum(w, 0, keepdims=True), (8, T)
        )
        return carry

    lax.fori_loop(0, 4, step, 0)


def near_stats_kernel(idx, lens, n0, n1, st, vt):
    place = idx[0]
    k = jnp.concatenate([n0[:, C : 2 * C], n1[:, C : 2 * C]], 0)
    vt[...] = turned(jnp.concatenate([n0[:, 2 * C : 3 * C], n1[:, 2 * C : 3 * C]], 0))
    q = n0[:128, :C]

    def step(c, carry):
        qc = q * lane_mask(c).astype(BF)
        bias = bias_of(
            slide(base_near(rows(T), place) + c, lens),
            slide(place * T + lanes(128) * 4 + c, lens),
        )
        w = jnp.exp2(nt(k, qc) * C1 + bias)
        top = pl.multiple_of(c * HD, 16)
        st[pl.ds(top, HD), :] = nn(vt[pl.ds(top, HD), :], w.astype(BF))
        st[pl.ds(pl.multiple_of(C + 8 * c, 8), 8), :] = jnp.broadcast_to(
            jnp.sum(w, 0, keepdims=True), (8, 128)
        )
        return carry

    lax.fori_loop(0, 4, step, 0)


def stacked(own, count):
    wide = own.astype(F32)
    parts = [wide * lane_mask(c) for c in range(4)]
    if count * 4 < 128:
        parts.append(jnp.zeros((128 - 4 * count, C), F32))
    return jnp.concatenate(parts, 0).astype(BF)


def wide_bias(base, count, rate, member, place, lens):
    shift = count.bit_length() - 1
    off = ((4 * member) & (rate - 1)) + (lanes(128) >> shift)
    q_pos = place * T + (lanes(128) & (count - 1)) * rate + off
    k_pos = base + off
    return bias_of(slide(k_pos, lens), slide(q_pos, lens))


def far_count(level):
    return (32, 16, base_mid) if level == 0 else (8, 64, base_far)


def half_pair(g0, g1, level, a, b):
    lo = 256 * level
    return jnp.concatenate([g0[lo : lo + 256, a:b], g1[lo : lo + 256, a:b]], 0)


def split3(x):
    hi = x.astype(BF).astype(F32)
    mid = (x - hi).astype(BF).astype(F32)
    lo = (x - hi - mid).astype(BF).astype(F32)
    return hi, mid, lo


def combine_kernel(idx, lens, x_ref, st_local, st_near, g0, g1, w_out, p0, p1, p2, p3, heads_t, full, own, aux_n, aux_m, aux_f, acc, heads):
    place, member = idx[0], idx[1]
    p = lanes(T)
    rh = row_head(C + 32)
    acc[...] = st_local[...] + spread(st_near[...], route_near(), (p & 3) == rh)
    for level in range(2):
        count, rate, base = far_count(level)
        shift = count.bit_length() - 1
        lo = 256 * level
        k = half_pair(g0, g1, level, C, 2 * C)
        vt = turned(half_pair(g0, g1, level, 2 * C, 3 * C))
        qbd = stacked(g0[lo : lo + max(count, 16), :C][:count], count)
        bias = wide_bias(base(rows(T), place), count, rate, member, place, lens)
        w = jnp.exp2(nt(k, qbd) * C1 + bias)
        lane_head = lanes(128) >> shift
        numer = nn(vt, w.astype(BF))
        totals = jnp.broadcast_to(jnp.sum(w, 0, keepdims=True), (32, 128))
        both = jnp.where(rh == lane_head, jnp.concatenate([numer, totals], 0), 0.0)
        route = route_mid() if level == 0 else route_far()
        ok = (p & (rate - 1)) == ((4 * member) & (rate - 1)) + rh
        acc[...] = acc[...] + spread(both, route, ok)
    gt = jnp.transpose(x_ref[:, 3 * C :].astype(F32))
    r8 = rows(8)
    pieces, mixes = [], []
    for c in range(4):
        total = acc[C + 8 * c : C + 8 * c + 1, :]
        mixed = acc[HD * c : HD * (c + 1), :] / total
        delta = jnp.sum(gt[HD * c : HD * (c + 1), :] * mixed, 0, keepdims=True)
        mixes.append(mixed)
        piece = jnp.zeros((8, T), F32)
        for j, part in enumerate(split3(jnp.log2(total)) + split3(delta)):
            piece = jnp.where(r8 == j, part, piece)
        pieces.append(piece)
    mixed = jnp.concatenate(mixes, 0)
    heads_t[...] = mixed.astype(BF)
    heads[...] = jnp.transpose(mixed).astype(BF)
    for j, out in enumerate((p0, p1, p2, p3)):
        at = pl.ds(pl.multiple_of((member ^ j) * 128, 128), 128)
        out[...] = nn(heads[at, :], w_out[...]).astype(BF)
    a32 = jnp.concatenate(pieces, 0)
    full[...] = a32
    rh32 = rows(32) >> 3
    for i, (rate, route, out, count) in enumerate(
        (
            (4, route_near(), aux_n, 128),
            (16, route_mid(), aux_m, 32),
            (64, route_far(), aux_f, 8),
        )
    ):
        ok = (p & (rate - 1)) == ((4 * member) & (rate - 1)) + rh32
        picked = nt(jnp.where(ok, a32, 0.0).astype(BF), route)
        own[32 * i : 32 * (i + 1), :] = picked
        square = jnp.concatenate([picked, jnp.zeros((96, 128), F32)], 0)
        out[...] = jnp.transpose(square)[:count].astype(BF)


def lse_of(a, c):
    return a[8 * c : 8 * c + 1] + a[8 * c + 1 : 8 * c + 2] + a[8 * c + 2 : 8 * c + 3]


def delta_of(a, c):
    return a[8 * c + 3 : 8 * c + 4] + a[8 * c + 4 : 8 * c + 5] + a[8 * c + 5 : 8 * c + 6]


def local_grads_kernel(idx, lens, x_ref, full, gqt, kv_ref, kt, bias, rowv):
    first = idx[0] * T
    q = x_ref[:, :C]
    k = x_ref[:, C : 2 * C]
    v = x_ref[:, 2 * C : 3 * C]
    g = x_ref[:, 3 * C :]
    kt[...] = turned(k)
    bias[...] = bias_of(slide(first + rows(T), lens), slide(first + lanes(T), lens))
    a = full[...]
    for c in range(4):
        rowv[c, 0:1, :] = lse_of(a, c)
        rowv[c, 1:2, :] = delta_of(a, c)
    kv_ref[...] = jnp.zeros((T, 2 * C), F32)

    def step(c, carry):
        m = lane_mask(c)
        mb = m.astype(BF)
        top = pl.multiple_of(c * HD, 16)
        w = jnp.exp2(nt(k, q * mb) * C1 + bias[...] - rowv[c, 0:1, :])
        low = w.astype(BF)
        ds = (w * (nt(v, g * mb) - rowv[c, 1:2, :])).astype(BF)
        kv_ref[:, :C] = kv_ref[:, :C] + nn(ds, q) * (m * FACTOR)
        kv_ref[:, C:] = kv_ref[:, C:] + nn(low, g) * m
        gqt[pl.ds(top, HD), :] = nn(kt[pl.ds(top, HD), :], ds)
        return carry

    lax.fori_loop(0, 4, step, 0)


def pack(keep_ref, send_ref, mine, parts):
    for j in range(8):
        block = mine ^ j
        out = keep_ref if j % 2 == 0 else send_ref
        lo = 96 * (j // 2)
        picked = [p[pl.ds(pl.multiple_of(block * n, 8), n), :] for p, n in parts]
        out[lo : lo + 96, :] = jnp.concatenate(picked, 0).astype(BF)


def query_grads_kernel(
    idx, lens, n0, n1, g0, g1, own, gqt, heads_t, branch, normed,
    gq_ref, term_q, term_out, kt, rowv, near_t,
):
    place, member = idx[0], idx[1]
    first = place * T
    o = own[...]
    for c in range(4):
        rowv[c, 2:3, 0:128] = lse_of(o[:32], c)
        rowv[c, 3:4, 0:128] = delta_of(o[:32], c)
    kn = jnp.concatenate([n0[:, C : 2 * C], n1[:, C : 2 * C]], 0)
    vn = jnp.concatenate([n0[:, 2 * C : 3 * C], n1[:, 2 * C : 3 * C]], 0)
    kt[...] = turned(kn)
    qn = n0[:128, :C]
    gn = n0[:128, 3 * C :]

    def near_step(c, carry):
        mb = lane_mask(c).astype(BF)
        top = pl.multiple_of(c * HD, 16)
        b = bias_of(
            slide(base_near(rows(T), place) + c, lens),
            slide(first + lanes(128) * 4 + c, lens),
        )
        w = jnp.exp2(nt(kn, qn * mb) * C1 + b - rowv[c, 2:3, 0:128])
        ds = (w * (nt(vn, gn * mb) - rowv[c, 3:4, 0:128])).astype(BF)
        near_t[pl.ds(top, HD), :] = nn(kt[pl.ds(top, HD), :], ds)
        return carry

    lax.fori_loop(0, 4, near_step, 0)
    p = lanes(T)
    rh = row_head(C)
    total = gqt[...] + spread(near_t[...], route_near(), (p & 3) == rh)
    for level in range(2):
        count, rate, base = far_count(level)
        shift = count.bit_length() - 1
        lo = 256 * level
        kk = half_pair(g0, g1, level, C, 2 * C)
        vv = half_pair(g0, g1, level, 2 * C, 3 * C)
        qbd = stacked(g0[lo : lo + max(count, 16), :C][:count], count)
        gbd = stacked(g0[lo : lo + max(count, 16), 3 * C :][:count], count)
        b = wide_bias(base(rows(T), place), count, rate, member, place, lens)
        lane_head = lanes(128) >> shift
        ol = o[32 + 32 * level : 64 + 32 * level]
        lse = jnp.zeros((1, 128), F32)
        delta = jnp.zeros((1, 128), F32)
        for c in range(4):
            lse = jnp.where(lane_head == c, lse_of(ol, c), lse)
            delta = jnp.where(lane_head == c, delta_of(ol, c), delta)
        w = jnp.where(lane_head < 4, jnp.exp2(nt(kk, qbd) * C1 + b - lse), 0.0)
        ds = (w * (nt(vv, gbd) - delta)).astype(BF)
        part = jnp.where(rh == lane_head, nn(turned(kk), ds), 0.0)
        route = route_mid() if level == 0 else route_far()
        ok = (p & (rate - 1)) == ((4 * member) & (rate - 1)) + rh
        total = total + spread(part, route, ok)
    total = total * FACTOR
    gq_ref[...] = jnp.transpose(total).astype(BF)
    term_out[...] = nn(heads_t[...], branch[...])
    term_q[...] = nn(total.astype(BF), normed[...])


def key_grads_kernel(
    idx, lens, n0, n1, g0, g1, a0, a1, kv, normed, term_q, term_out,
    gkv_ref, keep_ref, send_ref, rowv, sel, term,
):
    place, member = idx[0], idx[1]

    def aux_rows(level):
        lo = 256 * level
        both = jnp.concatenate([a0[lo : lo + 256, :], a1[lo : lo + 256, :]], 0)
        return jnp.transpose(both.astype(F32))

    near = aux_rows(0)
    for c in range(4):
        rowv[c, 0:1, :] = lse_of(near, c)
        rowv[c, 1:2, :] = delta_of(near, c)
    qn = jnp.concatenate([n0[:, :C], n1[:, :C]], 0)
    gn = jnp.concatenate([n0[:, 3 * C :], n1[:, 3 * C :]], 0)
    kn = n0[:128, C : 2 * C]
    vn = n0[:128, 2 * C : 3 * C]
    sel[...] = jnp.zeros((128, 2 * C), F32)

    def near_step(c, carry):
        m = lane_mask(c)
        mb = m.astype(BF)
        b = bias_of(
            slide(place * T + rows(128) * 4 + c, lens),
            slide(base_near(lanes(T), place) + c, lens),
        )
        w = jnp.exp2(nt(kn * mb, qn) * C1 + b - rowv[c, 0:1, :])
        low = w.astype(BF)
        ds = (w * (nt(vn * mb, gn) - rowv[c, 1:2, :])).astype(BF)
        sel[:, :C] = sel[:, :C] + nn(ds, qn) * m
        sel[:, C:] = sel[:, C:] + nn(low, gn) * m
        return carry

    lax.fori_loop(0, 4, near_step, 0)
    p = rows(T)
    lane_head8 = head_of(lanes(2 * C), 8) & 3
    scale = jnp.where(lanes(2 * C) < C, FACTOR, 1.0)

    def place_rows(x, rate, shift, count):
        take = jnp.where((rows(T, count) >> shift) == lanes(count, T), 1.0, 0.0).astype(BF)
        hi = x.astype(BF)
        lo = (x - hi.astype(F32)).astype(BF)
        ok = (p & (rate - 1)) == ((4 * member) & (rate - 1)) + lane_head8
        return jnp.where(ok, nn(take, hi) + nn(take, lo), 0.0)

    total = place_rows(sel[...], 4, 2, 128)
    for level in range(2):
        count, rate, base = far_count(level)
        shift = count.bit_length() - 1
        lo = 256 * level
        q = half_pair(g0, g1, level, 0, C)
        g = half_pair(g0, g1, level, 3 * C, 4 * C)
        kbd = stacked(g0[lo : lo + max(count, 16), C : 2 * C][:count], count)
        vbd = stacked(g0[lo : lo + max(count, 16), 2 * C : 3 * C][:count], count)
        row_c = rows(128) >> shift
        off = ((4 * member) & (rate - 1)) + row_c
        b = bias_of(
            slide(place * T + (rows(128) & (count - 1)) * rate + off, lens),
            slide(base(lanes(T), place) + off, lens),
        )
        aux = aux_rows(level + 1)
        lse = jnp.zeros((1, T), F32)
        delta = jnp.zeros((1, T), F32)
        for c in range(4):
            lse = jnp.where(row_c == c, lse_of(aux, c), lse)
            delta = jnp.where(row_c == c, delta_of(aux, c), delta)
        w = jnp.where(row_c < 4, jnp.exp2(nt(kbd, q) * C1 + b - lse), 0.0)
        ds = (w * (nt(vbd, g) - delta)).astype(BF)
        both = jnp.concatenate([nn(ds, q), nn(w.astype(BF), g)], 1)
        both = jnp.where(row_c == lane_head8, both, 0.0)
        merged = both[:count]
        for c in range(1, 4):
            merged = merged + both[c * count : (c + 1) * count]
        total = total + place_rows(
            jnp.concatenate([merged, jnp.zeros((128 - count, 2 * C), F32)], 0), rate, 4 if level == 0 else 6, 128
        )
    gkv = kv[...] + total * scale
    gkv_ref[...] = gkv.astype(BF)
    term[...] = nn(turned(gkv), normed[...])
    pack(keep_ref, send_ref, place & 7, ((term_q, 24), (term_out, 24), (term, 48)))


def back_kernel(gq, gkv, w, out):
    out[...] = (nn(gq[...], w[:C, :]) + nn(gkv[...], w[C:, :])).astype(BF)


def layer_kernel(idx, salt, p0, p1, p2, p3, out):
    drop = jnp.where(keep(salt[0], idx[0] * T + idx[1] * 128, 128), DROP, 0.0)
    proj = p0[...].astype(F32) + p1[...].astype(F32) + p2[...].astype(F32) + p3[...].astype(F32)
    out[...] = (proj * drop).astype(BF)


def tile_kernel(idx, tiles, grad, out):
    at = pl.ds(pl.multiple_of(idx[1] * 128, 128), 128)
    xhat, inv = standard(tiles[at, :])
    g = grad[...].astype(F32)
    mean = jnp.mean(g, -1, keepdims=True)
    cross = jnp.mean(g * xhat, -1, keepdims=True)
    out[...] = (inv * (g - mean - xhat * cross)).astype(BF)


def join_kernel(idx, t0, t1, t2, t3, out):
    for j, t in enumerate((t0, t1, t2, t3)):
        out[pl.ds(pl.multiple_of((idx[1] ^ j) * 128, 128), 128), :] = t[...]


def finish_kernel(scale, idx, s0, s1, gw, go):
    mine = idx[0] & 7
    for j in range(8):
        block = mine ^ j
        lo = 96 * (j // 2)
        src = s0 if j % 2 == 0 else s1
        wide = src[lo : lo + 96, :].astype(F32) * scale
        at = pl.ds(pl.multiple_of(block * 24, 8), 24)
        gw[at, :] = wide[:24]
        go[at, :] = wide[24:48]
        gw[pl.ds(pl.multiple_of(C + block * 48, 16), 48), :] = wide[48:]


def call(kernel, n_scalar, args, outs, scratch=(), flops=0):
    specs = [pl.BlockSpec(memory_space=pltpu.SMEM)] * n_scalar
    specs += [pl.BlockSpec(memory_space=pltpu.VMEM)] * (len(args) - n_scalar)
    return pl.pallas_call(
        kernel,
        in_specs=specs,
        out_specs=[pl.BlockSpec(memory_space=pltpu.VMEM)] * len(outs),
        out_shape=[jax.ShapeDtypeStruct(s, d) for s, d in outs],
        scratch_shapes=[pltpu.VMEM(s, d) for s, d in scratch],
        compiler_params=pltpu.CompilerParams(vmem_limit_bytes=40 * 2**20),
        cost_estimate=pl.CostEstimate(flops=flops, bytes_accessed=flops // 200, transcendentals=0),
    )(*args)


def shards(tiles, w_qkv, w_out, slide_lengths, drop_salt, cotangent):
    member = lax.axis_index("mp")
    place = lax.axis_index("seq")
    groups = lax.axis_size("seq")
    idx = jnp.stack([place, member]).astype(I32)

    def swap(x, mask):
        return lax.ppermute(x, "seq", [(i, i ^ mask) for i in range(groups)])

    def across(x, mask):
        return lax.ppermute(x, "mp", [(i, i ^ mask) for i in range(4)])

    def tie(a, b):
        return lax.optimization_barrier((a, b))

    cat = jnp.concatenate
    us = 10**9
    w_t = w_qkv.T

    (branch,) = call(branch_kernel, 2, (idx, drop_salt, cotangent), [((T, D), BF)], flops=3 * us)
    x, near, mid, far, normed = call(
        start_kernel, 1, (idx, tiles, w_t, w_out, branch),
        [((T, D), BF), ((128, D), BF), ((32, D), BF), ((8, D), BF), ((T, D), BF)], flops=4 * us,
    )
    got = swap(far, 32)
    got_n = swap(near, 2)
    (st_local,) = call(
        local_stats_kernel, 2, (idx, slide_lengths, x),
        [((C + 32, T), F32)], [((C, T), BF), ((T, T), F32)], flops=5 * us,
    )
    got, st_local = tie(got, st_local)
    far = cat([far, got], 0)
    n0 = cat([near, got_n], 0)
    n1 = swap(n0, 1)
    far = cat([far, swap(far, 16)], 0)
    got = swap(cat([mid, far], 0), 8)
    (st_near,) = call(
        near_stats_kernel, 2, (idx, slide_lengths, n0, n1),
        [((C + 32, 128), F32)], [((C, T), BF)], flops=2 * us,
    )
    got, st_near = tie(got, st_near)
    both = cat([mid, got[:32], far, got[32:]], 0)
    got = [both, swap(both, 2), swap(both, 4), swap(both, 6)]
    g0 = cat([b[:64] for b in got] + [b[64:] for b in got], 0)
    g1 = swap(g0, 1)

    p0, p1, p2, p3, heads_t, full, own, aux_n, aux_m, aux_f = call(
        combine_kernel, 2, (idx, slide_lengths, x, st_local, st_near, g0, g1, w_out),
        [((128, D), BF)] * 4
        + [((C, T), BF), ((32, T), F32), ((96, 128), F32), ((128, 128), BF), ((32, 128), BF), ((8, 128), BF)],
        [((C + 32, T), F32), ((T, C), BF)], flops=4 * us,
    )
    def wide(a):
        return a.astype(F32)

    def cut(part):
        return [part[96 * i : 96 * (i + 1)] for i in range(4)]

    def x_swaps(pieces):
        return [swap(pieces[i], 2 * i) for i in range(1, 4)]

    def x_sum(pieces, got):
        return (wide(pieces[0]) + (wide(got[0]) + wide(got[1])) + wide(got[2])).astype(BF)

    def plus(part, got):
        return (wide(part) + wide(got)).astype(BF)

    got = swap(aux_f, 32)
    p_in = [across(p1, 1), across(p3, 3), across(p2, 2)]
    gqt, kv = call(
        local_grads_kernel, 2, (idx, slide_lengths, x, full),
        [((C, T), F32), ((T, 2 * C), F32)],
        [((C, T), BF), ((T, T), F32), ((4, 8, T), F32)], flops=6 * us,
    )
    got, gqt = tie(got, gqt)
    far = cat([aux_f, got], 0)
    got = swap(far, 16)
    query = call(
        query_grads_kernel, 2,
        (idx, slide_lengths, n0, n1, g0, g1, own, gqt, heads_t, branch, normed),
        [((T, C), BF), ((C, D), F32), ((C, D), F32)],
        [((C, T), BF), ((4, 8, T), F32), ((C, 128), F32)], flops=6 * us,
    )
    got, ((gq, term_q, term_out), p_in) = tie(got, (query, p_in))
    (l0,) = call(layer_kernel, 2, (idx, drop_salt, p0, *p_in), [((128, D), BF)], flops=us)
    l_in = [across(l0, 1), across(l0, 2), across(l0, 3)]
    far = cat([far, got], 0)
    got = swap(cat([aux_m, far], 0), 8)
    both = cat([aux_m, got[:32], far, got[32:]], 0)
    first = swap(cat([both, aux_n], 0), 2)
    got = [both, first[:128], swap(both, 4), swap(both, 6)]
    a0 = cat([aux_n, first[128:]] + [b[:64] for b in got] + [b[64:] for b in got], 0)
    a1 = swap(a0, 1)

    key = call(
        key_grads_kernel, 2,
        (idx, slide_lengths, n0, n1, g0, g1, a0, a1, kv, normed, term_q, term_out),
        [((T, 2 * C), BF), ((384, D), BF), ((384, D), BF)],
        [((4, 8, T), F32), ((128, 2 * C), F32), ((2 * C, D), F32)], flops=5 * us,
    )
    (gkv, kept, sent), l_in = tie(key, l_in)
    got = swap(sent, 1)
    (back,) = call(back_kernel, 0, (gq, gkv, w_t), [((T, D), BF)], flops=us)
    got, back = tie(got, back)
    back = lax.psum_scatter(back, "mp", scatter_dimension=0, tiled=True)
    part = cut(plus(kept, got))
    part = x_sum(part, x_swaps(part))
    got = swap(part, 8)
    (layer_out,) = call(join_kernel, 1, (idx, l0, *l_in), [((T, D), BF)], flops=us)
    got, layer_out = tie(got, layer_out)
    part = plus(part, got)
    got, back = tie(swap(part, 16), back)
    part = plus(part, got)
    got = swap(part, 32)
    part = plus(part, got)
    got = x_swaps([part] * 4)
    (t0,) = call(tile_kernel, 1, (idx, tiles, back), [((128, D), BF)], flops=us)
    got, t_in = tie(got, [across(t0, j) for j in range(1, 4)])
    s0 = cat([part] + got, 0)
    s1 = swap(s0, 1)
    (tile_gradient,) = call(join_kernel, 1, (idx, t0, *t_in), [((T, D), BF)], flops=us)
    s1, tile_gradient = tie(s1, tile_gradient)
    scale = (T * groups) ** -0.5

    def finish(*refs):
        finish_kernel(scale, *refs)

    grad_w_t, grad_w_out = call(
        finish, 1, (idx, s0, s1), [((3 * C, D), F32), ((C, D), F32)], flops=us
    )
    return (layer_out, tile_gradient, grad_w_t.T, grad_w_out)


def solution(mesh):
    placed = (P("seq", None), P(None, "mp"), P("mp", None), P(), P(), P("seq", None))
    return jax.shard_map(
        shards,
        mesh=mesh,
        in_specs=placed,
        out_specs=(P("seq", None), P("seq", None), P(None, "mp"), P("mp", None)),
        check_vma=False,
    )
```

```python
import jax
import jax.numpy as jnp
from jax import lax
from jax.experimental import pallas as pl
from jax.experimental.pallas import tpu as pltpu
from jax.sharding import PartitionSpec as P

BF = jnp.bfloat16
F32 = jnp.float32
I32 = jnp.int32
T = 512
D = 768
HD = 48
C = 4 * HD
DROP = 1024.0 / 922.0
FACTOR = HD**-0.5
C1 = FACTOR * 1.4426950408889634
NEG = -1e30


def nt(a, b):
    return lax.dot_general(a, b, (((1,), (1,)), ((), ())), preferred_element_type=F32)


def nn(a, b):
    return lax.dot_general(a, b, (((1,), (0,)), ((), ())), preferred_element_type=F32)


def rows(n, m=1):
    return lax.broadcasted_iota(I32, (n, m), 0)


def lanes(m, n=1):
    return lax.broadcasted_iota(I32, (n, m), 1)


def head_of(x, top):
    total = jnp.zeros_like(x)
    for j in range(1, top):
        total = total + (x >= j * HD).astype(I32)
    return total


def lane_mask(c):
    col = lanes(C)
    return jnp.where((col >= c * HD) & (col < (c + 1) * HD), 1.0, 0.0)


def slide(pos, len_ref):
    e0 = len_ref[0]
    e1 = e0 + len_ref[1]
    e2 = e1 + len_ref[2]
    return (pos >= e0).astype(I32) + (pos >= e1).astype(I32) + (pos >= e2).astype(I32)


def bias_of(a, b):
    return jnp.where(a == b, 0.0, NEG)


def keep(salt, first, n):
    index = (first + rows(n, D)) * D + lanes(D, n)
    mixed = index * 747796405 + salt
    mixed = mixed ^ (mixed >> 13)
    mixed = mixed * 1274126177
    mixed = mixed ^ (mixed >> 16)
    return (mixed & 1023) >= 102


def standard(x):
    wide = x.astype(F32)
    centred = wide - jnp.mean(wide, -1, keepdims=True)
    inv = lax.rsqrt(jnp.mean(centred * centred, -1, keepdims=True) + 1e-05)
    return centred * inv, inv


def off_near(s):
    return ((s & 1) << 1) | (s >> 1)


def off_mid(s):
    return ((s & 1) << 3) | (s & 6) | (s >> 3)


def base_near(r, place):
    return (place ^ off_near(r >> 7)) * T + (r & 127) * 4


def base_mid(r, place):
    return (place ^ off_mid(r >> 5)) * T + (r & 31) * 16


def base_far(r, place):
    s = r >> 3
    z = place >> 3
    gray = (z ^ (z >> 1)) ^ (((s & 1) << 2) | (s & 2) | ((s >> 2) & 1))
    z = gray ^ (gray >> 1) ^ (gray >> 2)
    low = (place & 7) ^ (((s >> 2) & 6) | (s >> 5))
    return ((z << 3) | low) * T + (r & 7) * 64


def route_near():
    return jnp.where((lanes(T, 128) >> 2) == rows(128, T), 1.0, 0.0).astype(BF)


def route_mid():
    return jnp.where((lanes(T, 128) >> 4) == (rows(128, T) & 31), 1.0, 0.0).astype(BF)


def route_far():
    r = rows(128, T)
    return jnp.where(((lanes(T, 128) >> 6) == (r & 7)) & (r < 32), 1.0, 0.0).astype(BF)


def spread(a, route, ok):
    half = a * 0.5
    hi = half.astype(BF)
    lo = (half - hi.astype(F32)).astype(BF)
    out = (nn(hi, route) + nn(lo, route)) * 2.0
    return jnp.where(ok, out, 0.0)


def row_head(n):
    r = rows(n)
    h = head_of(jnp.minimum(r, C - 1), 4)
    return jnp.where(r < C, h, (r - C) >> 3)


def turned(x):
    return jnp.transpose(x.astype(F32)).astype(BF)


def branch_kernel(idx, salt, cot, branch):
    drop = jnp.where(keep(salt[0], idx[0] * T, T), DROP, 0.0)
    branch[...] = (cot[...].astype(F32) * drop).astype(BF)


def start_kernel(idx, tiles, w, w_out, branch, x_ref, near, mid, far, normed_ref):
    member = idx[1]
    xhat, _ = standard(tiles[...])
    normed = xhat.astype(BF)
    normed_ref[...] = normed
    x_ref[:, : 3 * C] = nt(normed, w[...]).astype(BF)
    x_ref[:, 3 * C :] = nt(branch[...], w_out[...]).astype(BF)
    x = x_ref[...].astype(F32)
    lane_head = head_of(lanes(D), 16) & 3
    p = rows(T)
    for out, count, rate, shift in ((near, 128, 4, 2), (mid, 32, 16, 4), (far, 8, 64, 6)):
        first = (4 * member) & (rate - 1)
        chosen = jnp.where((p & (rate - 1)) == first + lane_head, x, 0.0).astype(BF)
        n = max(count, 16)
        pick = jnp.where((lanes(T, n) >> shift) == rows(n, T), 1.0, 0.0).astype(BF)
        out[...] = nn(pick, chosen)[:count].astype(BF)


def local_stats_kernel(idx, lens, x_ref, st, vt, bias):
    place = idx[0]
    first = place * T
    q = x_ref[:, :C]
    k = x_ref[:, C : 2 * C]
    vt[...] = turned(x_ref[:, 2 * C : 3 * C])
    bias[...] = bias_of(slide(first + rows(T), lens), slide(first + lanes(T), lens))

    def step(c, carry):
        qc = q * lane_mask(c).astype(BF)
        w = jnp.exp2(nt(k, qc) * C1 + bias[...])
        top = pl.multiple_of(c * HD, 16)
        st[pl.ds(top, HD), :] = nn(vt[pl.ds(top, HD), :], w.astype(BF))
        st[pl.ds(pl.multiple_of(C + 8 * c, 8), 8), :] = jnp.broadcast_to(
            jnp.sum(w, 0, keepdims=True), (8, T)
        )
        return carry

    lax.fori_loop(0, 4, step, 0, unroll=True)


def near_stats_kernel(idx, lens, n0, n1, st, vt):
    place = idx[0]
    k = jnp.concatenate([n0[:, C : 2 * C], n1[:, C : 2 * C]], 0)
    vt[...] = turned(jnp.concatenate([n0[:, 2 * C : 3 * C], n1[:, 2 * C : 3 * C]], 0))
    q = n0[:128, :C]

    def step(c, carry):
        qc = q * lane_mask(c).astype(BF)
        bias = bias_of(
            slide(base_near(rows(T), place) + c, lens),
            slide(place * T + lanes(128) * 4 + c, lens),
        )
        w = jnp.exp2(nt(k, qc) * C1 + bias)
        top = pl.multiple_of(c * HD, 16)
        st[pl.ds(top, HD), :] = nn(vt[pl.ds(top, HD), :], w.astype(BF))
        st[pl.ds(pl.multiple_of(C + 8 * c, 8), 8), :] = jnp.broadcast_to(
            jnp.sum(w, 0, keepdims=True), (8, 128)
        )
        return carry

    lax.fori_loop(0, 4, step, 0, unroll=True)


def stacked(own, count):
    wide = own.astype(F32)
    parts = [wide * lane_mask(c) for c in range(4)]
    if count * 4 < 128:
        parts.append(jnp.zeros((128 - 4 * count, C), F32))
    return jnp.concatenate(parts, 0).astype(BF)


def wide_bias(base, count, rate, member, place, lens):
    shift = count.bit_length() - 1
    off = ((4 * member) & (rate - 1)) + (lanes(128) >> shift)
    q_pos = place * T + (lanes(128) & (count - 1)) * rate + off
    k_pos = base + off
    return bias_of(slide(k_pos, lens), slide(q_pos, lens))


def far_count(level):
    return (32, 16, base_mid) if level == 0 else (8, 64, base_far)


def half_pair(g0, g1, level, a, b):
    lo = 256 * level
    return jnp.concatenate([g0[lo : lo + 256, a:b], g1[lo : lo + 256, a:b]], 0)


def split3(x):
    hi = x.astype(BF).astype(F32)
    mid = (x - hi).astype(BF).astype(F32)
    lo = (x - hi - mid).astype(BF).astype(F32)
    return hi, mid, lo


def combine_kernel(idx, lens, x_ref, st_local, st_near, g0, g1, heads, heads_t, full, own, aux_n, aux_m, aux_f, acc):
    place, member = idx[0], idx[1]
    p = lanes(T)
    rh = row_head(C + 32)
    acc[...] = st_local[...] + spread(st_near[...], route_near(), (p & 3) == rh)
    for level in range(2):
        count, rate, base = far_count(level)
        shift = count.bit_length() - 1
        lo = 256 * level
        k = half_pair(g0, g1, level, C, 2 * C)
        vt = turned(half_pair(g0, g1, level, 2 * C, 3 * C))
        qbd = stacked(g0[lo : lo + max(count, 16), :C][:count], count)
        bias = wide_bias(base(rows(T), place), count, rate, member, place, lens)
        w = jnp.exp2(nt(k, qbd) * C1 + bias)
        lane_head = lanes(128) >> shift
        numer = nn(vt, w.astype(BF))
        totals = jnp.broadcast_to(jnp.sum(w, 0, keepdims=True), (32, 128))
        both = jnp.where(rh == lane_head, jnp.concatenate([numer, totals], 0), 0.0)
        route = route_mid() if level == 0 else route_far()
        ok = (p & (rate - 1)) == ((4 * member) & (rate - 1)) + rh
        acc[...] = acc[...] + spread(both, route, ok)
    gt = jnp.transpose(x_ref[:, 3 * C :].astype(F32))
    r8 = rows(8)
    pieces, mixes = [], []
    for c in range(4):
        total = acc[C + 8 * c : C + 8 * c + 1, :]
        mixed = acc[HD * c : HD * (c + 1), :] / total
        delta = jnp.sum(gt[HD * c : HD * (c + 1), :] * mixed, 0, keepdims=True)
        mixes.append(mixed)
        piece = jnp.zeros((8, T), F32)
        for j, part in enumerate(split3(jnp.log2(total)) + split3(delta)):
            piece = jnp.where(r8 == j, part, piece)
        pieces.append(piece)
    mixed = jnp.concatenate(mixes, 0)
    heads_t[...] = mixed.astype(BF)
    heads[...] = jnp.transpose(mixed).astype(BF)
    a32 = jnp.concatenate(pieces, 0)
    full[...] = a32
    rh32 = rows(32) >> 3
    for i, (rate, route, out, count) in enumerate(
        (
            (4, route_near(), aux_n, 128),
            (16, route_mid(), aux_m, 32),
            (64, route_far(), aux_f, 8),
        )
    ):
        ok = (p & (rate - 1)) == ((4 * member) & (rate - 1)) + rh32
        picked = nt(jnp.where(ok, a32, 0.0).astype(BF), route)
        own[32 * i : 32 * (i + 1), :] = picked
        square = jnp.concatenate([picked, jnp.zeros((96, 128), F32)], 0)
        out[...] = jnp.transpose(square)[:count].astype(BF)


def lse_of(a, c):
    return a[8 * c : 8 * c + 1] + a[8 * c + 1 : 8 * c + 2] + a[8 * c + 2 : 8 * c + 3]


def delta_of(a, c):
    return a[8 * c + 3 : 8 * c + 4] + a[8 * c + 4 : 8 * c + 5] + a[8 * c + 5 : 8 * c + 6]


def local_grads_kernel(idx, lens, x_ref, full, gqt, kv_ref, kt, bias, rowv):
    first = idx[0] * T
    q = x_ref[:, :C]
    k = x_ref[:, C : 2 * C]
    v = x_ref[:, 2 * C : 3 * C]
    g = x_ref[:, 3 * C :]
    kt[...] = turned(k)
    bias[...] = bias_of(slide(first + rows(T), lens), slide(first + lanes(T), lens))
    a = full[...]
    for c in range(4):
        rowv[c, 0:1, :] = lse_of(a, c)
        rowv[c, 1:2, :] = delta_of(a, c)
    kv_ref[...] = jnp.zeros((T, 2 * C), F32)

    def step(c, carry):
        m = lane_mask(c)
        mb = m.astype(BF)
        top = pl.multiple_of(c * HD, 16)
        w = jnp.exp2(nt(k, q * mb) * C1 + bias[...] - rowv[c, 0:1, :])
        low = w.astype(BF)
        ds = (w * (nt(v, g * mb) - rowv[c, 1:2, :])).astype(BF)
        kv_ref[:, :C] = kv_ref[:, :C] + nn(ds, q) * (m * FACTOR)
        kv_ref[:, C:] = kv_ref[:, C:] + nn(low, g) * m
        gqt[pl.ds(top, HD), :] = nn(kt[pl.ds(top, HD), :], ds)
        return carry

    lax.fori_loop(0, 4, step, 0, unroll=True)


def pack(keep_ref, send_ref, mine, parts):
    for j in range(8):
        block = mine ^ j
        out = keep_ref if j % 2 == 0 else send_ref
        lo = 96 * (j // 2)
        picked = [p[pl.ds(pl.multiple_of(block * n, 8), n), :] for p, n in parts]
        out[lo : lo + 96, :] = jnp.concatenate(picked, 0).astype(BF)


def query_grads_kernel(
    idx, lens, n0, n1, g0, g1, own, gqt, heads_t, branch, normed,
    gq_ref, term_q, term_out, kt, rowv, near_t,
):
    place, member = idx[0], idx[1]
    first = place * T
    o = own[...]
    for c in range(4):
        rowv[c, 2:3, 0:128] = lse_of(o[:32], c)
        rowv[c, 3:4, 0:128] = delta_of(o[:32], c)
    kn = jnp.concatenate([n0[:, C : 2 * C], n1[:, C : 2 * C]], 0)
    vn = jnp.concatenate([n0[:, 2 * C : 3 * C], n1[:, 2 * C : 3 * C]], 0)
    kt[...] = turned(kn)
    qn = n0[:128, :C]
    gn = n0[:128, 3 * C :]

    def near_step(c, carry):
        mb = lane_mask(c).astype(BF)
        top = pl.multiple_of(c * HD, 16)
        b = bias_of(
            slide(base_near(rows(T), place) + c, lens),
            slide(first + lanes(128) * 4 + c, lens),
        )
        w = jnp.exp2(nt(kn, qn * mb) * C1 + b - rowv[c, 2:3, 0:128])
        ds = (w * (nt(vn, gn * mb) - rowv[c, 3:4, 0:128])).astype(BF)
        near_t[pl.ds(top, HD), :] = nn(kt[pl.ds(top, HD), :], ds)
        return carry

    lax.fori_loop(0, 4, near_step, 0, unroll=True)
    p = lanes(T)
    rh = row_head(C)
    total = gqt[...] + spread(near_t[...], route_near(), (p & 3) == rh)
    for level in range(2):
        count, rate, base = far_count(level)
        shift = count.bit_length() - 1
        lo = 256 * level
        kk = half_pair(g0, g1, level, C, 2 * C)
        vv = half_pair(g0, g1, level, 2 * C, 3 * C)
        qbd = stacked(g0[lo : lo + max(count, 16), :C][:count], count)
        gbd = stacked(g0[lo : lo + max(count, 16), 3 * C :][:count], count)
        b = wide_bias(base(rows(T), place), count, rate, member, place, lens)
        lane_head = lanes(128) >> shift
        ol = o[32 + 32 * level : 64 + 32 * level]
        lse = jnp.zeros((1, 128), F32)
        delta = jnp.zeros((1, 128), F32)
        for c in range(4):
            lse = jnp.where(lane_head == c, lse_of(ol, c), lse)
            delta = jnp.where(lane_head == c, delta_of(ol, c), delta)
        w = jnp.where(lane_head < 4, jnp.exp2(nt(kk, qbd) * C1 + b - lse), 0.0)
        ds = (w * (nt(vv, gbd) - delta)).astype(BF)
        part = jnp.where(rh == lane_head, nn(turned(kk), ds), 0.0)
        route = route_mid() if level == 0 else route_far()
        ok = (p & (rate - 1)) == ((4 * member) & (rate - 1)) + rh
        total = total + spread(part, route, ok)
    total = total * FACTOR
    gq_ref[...] = jnp.transpose(total).astype(BF)
    term_out[...] = nn(heads_t[...], branch[...])
    term_q[...] = nn(total.astype(BF), normed[...])


def key_grads_kernel(
    idx, lens, n0, n1, g0, g1, a0, a1, kv, normed, term_q, term_out,
    gkv_ref, keep_ref, send_ref, rowv, sel, term,
):
    place, member = idx[0], idx[1]

    def aux_rows(level):
        lo = 256 * level
        both = jnp.concatenate([a0[lo : lo + 256, :], a1[lo : lo + 256, :]], 0)
        return jnp.transpose(both.astype(F32))

    near = aux_rows(0)
    for c in range(4):
        rowv[c, 0:1, :] = lse_of(near, c)
        rowv[c, 1:2, :] = delta_of(near, c)
    qn = jnp.concatenate([n0[:, :C], n1[:, :C]], 0)
    gn = jnp.concatenate([n0[:, 3 * C :], n1[:, 3 * C :]], 0)
    kn = n0[:128, C : 2 * C]
    vn = n0[:128, 2 * C : 3 * C]
    sel[...] = jnp.zeros((128, 2 * C), F32)

    def near_step(c, carry):
        m = lane_mask(c)
        mb = m.astype(BF)
        b = bias_of(
            slide(place * T + rows(128) * 4 + c, lens),
            slide(base_near(lanes(T), place) + c, lens),
        )
        w = jnp.exp2(nt(kn * mb, qn) * C1 + b - rowv[c, 0:1, :])
        low = w.astype(BF)
        ds = (w * (nt(vn * mb, gn) - rowv[c, 1:2, :])).astype(BF)
        sel[:, :C] = sel[:, :C] + nn(ds, qn) * m
        sel[:, C:] = sel[:, C:] + nn(low, gn) * m
        return carry

    lax.fori_loop(0, 4, near_step, 0, unroll=True)
    p = rows(T)
    lane_head8 = head_of(lanes(2 * C), 8) & 3
    scale = jnp.where(lanes(2 * C) < C, FACTOR, 1.0)

    def place_rows(x, rate, shift, count):
        take = jnp.where((rows(T, count) >> shift) == lanes(count, T), 1.0, 0.0).astype(BF)
        hi = x.astype(BF)
        lo = (x - hi.astype(F32)).astype(BF)
        ok = (p & (rate - 1)) == ((4 * member) & (rate - 1)) + lane_head8
        return jnp.where(ok, nn(take, hi) + nn(take, lo), 0.0)

    total = place_rows(sel[...], 4, 2, 128)
    for level in range(2):
        count, rate, base = far_count(level)
        shift = count.bit_length() - 1
        lo = 256 * level
        q = half_pair(g0, g1, level, 0, C)
        g = half_pair(g0, g1, level, 3 * C, 4 * C)
        kbd = stacked(g0[lo : lo + max(count, 16), C : 2 * C][:count], count)
        vbd = stacked(g0[lo : lo + max(count, 16), 2 * C : 3 * C][:count], count)
        row_c = rows(128) >> shift
        off = ((4 * member) & (rate - 1)) + row_c
        b = bias_of(
            slide(place * T + (rows(128) & (count - 1)) * rate + off, lens),
            slide(base(lanes(T), place) + off, lens),
        )
        aux = aux_rows(level + 1)
        lse = jnp.zeros((1, T), F32)
        delta = jnp.zeros((1, T), F32)
        for c in range(4):
            lse = jnp.where(row_c == c, lse_of(aux, c), lse)
            delta = jnp.where(row_c == c, delta_of(aux, c), delta)
        w = jnp.where(row_c < 4, jnp.exp2(nt(kbd, q) * C1 + b - lse), 0.0)
        ds = (w * (nt(vbd, g) - delta)).astype(BF)
        both = jnp.concatenate([nn(ds, q), nn(w.astype(BF), g)], 1)
        both = jnp.where(row_c == lane_head8, both, 0.0)
        merged = both[:count]
        for c in range(1, 4):
            merged = merged + both[c * count : (c + 1) * count]
        total = total + place_rows(
            jnp.concatenate([merged, jnp.zeros((128 - count, 2 * C), F32)], 0), rate, 4 if level == 0 else 6, 128
        )
    gkv = kv[...] + total * scale
    gkv_ref[...] = gkv.astype(BF)
    term[...] = nn(turned(gkv), normed[...])
    pack(keep_ref, send_ref, place & 7, ((term_q, 24), (term_out, 24), (term, 48)))


def back_kernel(idx, gq, gkv, w, b0, b1, b2, b3):
    for j, out in enumerate((b0, b1, b2, b3)):
        at = pl.ds(pl.multiple_of((idx[1] ^ j) * 128, 128), 128)
        out[...] = (nn(gq[at, :], w[:C, :]) + nn(gkv[at, :], w[C:, :])).astype(BF)


def layer_kernel(idx, salt, h0, h1, h2, h3, w0, w1, w2, w3, out):
    drop = jnp.where(keep(salt[0], idx[0] * T, T), DROP, 0.0)
    first = nn(h0[...], w0[...]) + nn(h1[...], w1[...])
    second = nn(h2[...], w2[...]) + nn(h3[...], w3[...])
    out[...] = ((first + second) * drop).astype(BF)


def tile_kernel(idx, tiles, b0, b1, b2, b3, out):
    at = pl.ds(pl.multiple_of(idx[1] * 128, 128), 128)
    xhat, inv = standard(tiles[at, :])
    g = b0[...].astype(F32) + b1[...].astype(F32) + b2[...].astype(F32) + b3[...].astype(F32)
    mean = jnp.mean(g, -1, keepdims=True)
    cross = jnp.mean(g * xhat, -1, keepdims=True)
    out[...] = (inv * (g - mean - xhat * cross)).astype(BF)


def join_kernel(idx, t0, t1, t2, t3, out, sems):
    copies = [
        pltpu.make_async_copy(
            t, out.at[pl.ds(pl.multiple_of((idx[1] ^ j) * 128, 128), 128), :], sems.at[j]
        )
        for j, t in enumerate((t0, t1, t2, t3))
    ]
    for copy in copies:
        copy.start()
    for copy in copies:
        copy.wait()


def finish_kernel(scale, idx, s0, s1, gw, go, wide, sems):
    mine = idx[0] & 7
    copies = []
    for j in range(8):
        block = mine ^ j
        lo = 96 * (j // 2)
        src = s0 if j % 2 == 0 else s1
        wide[j] = src[lo : lo + 96, :].astype(F32) * scale
        narrow = pl.ds(pl.multiple_of(block * 24, 8), 24)
        broad = pl.ds(pl.multiple_of(C + block * 48, 16), 48)
        for i, (part, dst) in enumerate(
            (
                (wide.at[j, 0:24, :], gw.at[narrow, :]),
                (wide.at[j, 24:48, :], go.at[narrow, :]),
                (wide.at[j, 48:96, :], gw.at[broad, :]),
            )
        ):
            copy = pltpu.make_async_copy(part, dst, sems.at[3 * j + i])
            copy.start()
            copies.append(copy)
    for copy in copies:
        copy.wait()


def call(kernel, n_scalar, args, outs, scratch=(), flops=0, sems=0):
    specs = [pl.BlockSpec(memory_space=pltpu.SMEM)] * n_scalar
    specs += [pl.BlockSpec(memory_space=pltpu.VMEM)] * (len(args) - n_scalar)
    return pl.pallas_call(
        kernel,
        in_specs=specs,
        out_specs=[pl.BlockSpec(memory_space=pltpu.HBM if sems else pltpu.VMEM)] * len(outs),
        out_shape=[jax.ShapeDtypeStruct(s, d) for s, d in outs],
        scratch_shapes=[pltpu.VMEM(s, d) for s, d in scratch]
        + ([pltpu.SemaphoreType.DMA((sems,))] if sems else []),
        compiler_params=pltpu.CompilerParams(vmem_limit_bytes=40 * 2**20),
        cost_estimate=pl.CostEstimate(flops=flops, bytes_accessed=flops // 200, transcendentals=0),
    )(*args)


def shards(tiles, w_qkv, w_out, slide_lengths, drop_salt, cotangent):
    member = lax.axis_index("mp")
    place = lax.axis_index("seq")
    groups = lax.axis_size("seq")
    idx = jnp.stack([place, member]).astype(I32)

    def swap(x, mask):
        return lax.ppermute(x, "seq", [(i, i ^ mask) for i in range(groups)])

    def along(i, bit):
        gray = (i >> 3) ^ (i >> 4) ^ bit
        return (gray ^ (gray >> 1) ^ (gray >> 2)) << 3 | i & 7

    def z_swap(x, bit):
        return lax.ppermute(x, "seq", [(i, along(i, bit)) for i in range(groups)])

    def across(x, mask):
        return lax.ppermute(x, "mp", [(i, i ^ mask) for i in range(4)])

    def tie(a, b):
        return lax.optimization_barrier((a, b))

    cat = jnp.concatenate
    us = 10**9
    w_t = w_qkv.T
    w_in = [across(w_out, j) for j in range(1, 4)]

    (branch,) = call(branch_kernel, 2, (idx, drop_salt, cotangent), [((T, D), BF)], flops=3 * us)
    x, near, mid, far, normed = call(
        start_kernel, 1, (idx, tiles, w_t, w_out, branch),
        [((T, D), BF), ((128, D), BF), ((32, D), BF), ((8, D), BF), ((T, D), BF)], flops=4 * us,
    )
    got = z_swap(far, 4)
    got_n = swap(near, 2)
    (st_local,) = call(
        local_stats_kernel, 2, (idx, slide_lengths, x),
        [((C + 32, T), F32)], [((C, T), BF), ((T, T), F32)], flops=5 * us,
    )
    (got, got_n), st_local = tie((got, got_n), st_local)
    far = cat([far, got], 0)
    n0 = cat([near, got_n], 0)
    n1 = swap(n0, 1)
    got, w_in = tie(z_swap(far, 2), w_in)
    far = cat([far, got], 0)
    got = swap(cat([mid, far], 0), 8)
    (st_near,) = call(
        near_stats_kernel, 2, (idx, slide_lengths, n0, n1),
        [((C + 32, 128), F32)], [((C, T), BF)], flops=2 * us,
    )
    got, st_near = tie(got, st_near)
    both = cat([mid, got[:32], far, got[32:]], 0)
    got = [both, swap(both, 2), swap(both, 4), swap(both, 6)]
    g0 = cat([b[:64] for b in got] + [b[64:] for b in got], 0)
    g1 = swap(g0, 1)

    heads, heads_t, full, own, aux_n, aux_m, aux_f = call(
        combine_kernel, 2, (idx, slide_lengths, x, st_local, st_near, g0, g1),
        [((T, C), BF), ((C, T), BF), ((32, T), F32), ((96, 128), F32), ((128, 128), BF), ((32, 128), BF), ((8, 128), BF)],
        [((C + 32, T), F32)], flops=4 * us,
    )
    def wide(a):
        return a.astype(F32)

    def cut(part):
        return [part[96 * i : 96 * (i + 1)] for i in range(4)]

    def x_swaps(pieces):
        return [swap(pieces[i], 2 * i) for i in range(1, 4)]

    def x_sum(pieces, got):
        return (wide(pieces[0]) + (wide(got[0]) + wide(got[1])) + wide(got[2])).astype(BF)

    def plus(part, got):
        return (wide(part) + wide(got)).astype(BF)

    got = z_swap(aux_f, 4)
    p_in = [across(heads, j) for j in range(1, 4)]
    gqt, kv = call(
        local_grads_kernel, 2, (idx, slide_lengths, x, full),
        [((C, T), F32), ((T, 2 * C), F32)],
        [((C, T), BF), ((T, T), F32), ((4, 8, T), F32)], flops=6 * us,
    )
    got, gqt = tie(got, gqt)
    far = cat([aux_f, got], 0)
    got = z_swap(far, 2)
    query = call(
        query_grads_kernel, 2,
        (idx, slide_lengths, n0, n1, g0, g1, own, gqt, heads_t, branch, normed),
        [((T, C), BF), ((C, D), F32), ((C, D), F32)],
        [((C, T), BF), ((4, 8, T), F32), ((C, 128), F32)], flops=6 * us,
    )
    got, ((gq, term_q, term_out), p_in) = tie(got, (query, p_in))
    far = cat([far, got], 0)
    got = swap(cat([aux_m, far], 0), 8)
    both = cat([aux_m, got[:32], far, got[32:]], 0)
    first, got = tie(swap(cat([both, aux_n], 0), 2), [swap(both, 4), swap(both, 6)])
    got = [both, first[:128]] + got
    a0 = cat([aux_n, first[128:]] + [b[:64] for b in got] + [b[64:] for b in got], 0)
    a1 = swap(a0, 1)

    key = call(
        key_grads_kernel, 2,
        (idx, slide_lengths, n0, n1, g0, g1, a0, a1, kv, normed, term_q, term_out),
        [((T, 2 * C), BF), ((384, D), BF), ((384, D), BF)],
        [((4, 8, T), F32), ((128, 2 * C), F32), ((2 * C, D), F32)], flops=5 * us,
    )
    gkv, kept, sent = key
    got = swap(sent, 1)
    back = call(back_kernel, 1, (idx, gq, gkv, w_t), [((128, D), BF)] * 4, flops=us)
    got, (b0, b1, b2, b3) = tie(got, back)
    part = cut(plus(kept, got))
    got = x_swaps(part)
    b_in = [across(b1, 1), across(b3, 3), across(b2, 2)]
    part = x_sum(part, got)
    got = swap(part, 8)
    (layer_out,) = call(
        layer_kernel, 2, (idx, drop_salt, heads, *p_in, w_out, *w_in), [((T, D), BF)], flops=2 * us
    )
    got, layer_out = tie(got, layer_out)
    part = plus(part, got)
    got = z_swap(part, 2)
    (t0,) = call(tile_kernel, 1, (idx, tiles, b0, *b_in), [((128, D), BF)], flops=us)
    got, t0 = tie(got, t0)
    part = plus(part, got)
    got = z_swap(part, 4)
    t_in = [across(t0, j) for j in range(1, 4)]
    part = plus(part, got)
    (tile_gradient,) = call(join_kernel, 1, (idx, t0, *t_in), [((T, D), BF)], flops=us, sems=4)
    got, tile_gradient = tie(x_swaps([part] * 4), tile_gradient)
    s0 = cat([part] + got, 0)
    s1 = swap(s0, 1)
    scale = (T * groups) ** -0.5

    def finish(*refs):
        finish_kernel(scale, *refs)

    grad_w_t, grad_w_out = call(
        finish, 1, (idx, s0, s1), [((3 * C, D), F32), ((C, D), F32)], [((8, 96, D), F32)], flops=us, sems=24
    )
    return (layer_out, tile_gradient, grad_w_t.T, grad_w_out)


def solution(mesh):
    placed = (P("seq", None), P(None, "mp"), P("mp", None), P(), P(), P("seq", None))
    return jax.shard_map(
        shards,
        mesh=mesh,
        in_specs=placed,
        out_specs=(P("seq", None), P("seq", None), P(None, "mp"), P("mp", None)),
        check_vma=False,
    )
```

```python
import jax
import jax.numpy as jnp
from jax import lax
from jax.experimental import pallas as pl
from jax.experimental.pallas import tpu as pltpu
from jax.sharding import PartitionSpec as P

BF = jnp.bfloat16
F32 = jnp.float32
I32 = jnp.int32
T = 512
D = 768
HD = 48
C = 4 * HD
DROP = 1024.0 / 922.0
FACTOR = HD**-0.5
C1 = FACTOR * 1.4426950408889634
NEG = -1e30


def nt(a, b):
    return lax.dot_general(a, b, (((1,), (1,)), ((), ())), preferred_element_type=F32)


def nn(a, b):
    return lax.dot_general(a, b, (((1,), (0,)), ((), ())), preferred_element_type=F32)


def rows(n, m=1):
    return lax.broadcasted_iota(I32, (n, m), 0)


def lanes(m, n=1):
    return lax.broadcasted_iota(I32, (n, m), 1)


def head_of(x, top):
    total = jnp.zeros_like(x)
    for j in range(1, top):
        total = total + (x >= j * HD).astype(I32)
    return total


def lane_mask(c):
    col = lanes(C)
    return jnp.where((col >= c * HD) & (col < (c + 1) * HD), 1.0, 0.0)


def slide(pos, len_ref):
    e0 = len_ref[0]
    e1 = e0 + len_ref[1]
    e2 = e1 + len_ref[2]
    return (pos >= e0).astype(I32) + (pos >= e1).astype(I32) + (pos >= e2).astype(I32)


def bias_of(a, b):
    return jnp.where(a == b, 0.0, NEG)


def keep(salt, first, n):
    index = (first + rows(n, D)) * D + lanes(D, n)
    mixed = index * 747796405 + salt
    mixed = mixed ^ (mixed >> 13)
    mixed = mixed * 1274126177
    mixed = mixed ^ (mixed >> 16)
    return (mixed & 1023) >= 102


def standard(x):
    wide = x.astype(F32)
    centred = wide - jnp.mean(wide, -1, keepdims=True)
    inv = lax.rsqrt(jnp.mean(centred * centred, -1, keepdims=True) + 1e-05)
    return centred * inv, inv


def off_near(s):
    return ((s & 1) << 1) | (s >> 1)


def off_mid(s):
    return ((s & 1) << 3) | (s & 6) | (s >> 3)


def base_near(r, place):
    return (place ^ off_near(r >> 7)) * T + (r & 127) * 4


def base_mid(r, place):
    return (place ^ off_mid(r >> 5)) * T + (r & 31) * 16


def base_far(r, place):
    s = r >> 3
    z = place >> 3
    gray = (z ^ (z >> 1)) ^ (((s & 1) << 2) | (s & 2) | ((s >> 2) & 1))
    z = gray ^ (gray >> 1) ^ (gray >> 2)
    low = (place & 7) ^ (((s >> 2) & 6) | (s >> 5))
    return ((z << 3) | low) * T + (r & 7) * 64


def route_near():
    return jnp.where((lanes(T, 128) >> 2) == rows(128, T), 1.0, 0.0).astype(BF)


def route_mid():
    return jnp.where((lanes(T, 128) >> 4) == (rows(128, T) & 31), 1.0, 0.0).astype(BF)


def route_far():
    r = rows(128, T)
    return jnp.where(((lanes(T, 128) >> 6) == (r & 7)) & (r < 32), 1.0, 0.0).astype(BF)


def spread(a, route, ok):
    half = a * 0.5
    hi = half.astype(BF)
    lo = (half - hi.astype(F32)).astype(BF)
    out = (nn(hi, route) + nn(lo, route)) * 2.0
    return jnp.where(ok, out, 0.0)


def row_head(n):
    r = rows(n)
    h = head_of(jnp.minimum(r, C - 1), 4)
    return jnp.where(r < C, h, (r - C) >> 3)


def turned(x):
    return jnp.transpose(x.astype(F32)).astype(BF)


def drop_kernel(idx, salt, drop):
    drop[...] = jnp.where(keep(salt[0], idx[0] * T, T), DROP, 0.0)


def start_kernel(idx, tiles, w, w_out, cot, drop, x_ref, near, mid, far, normed_ref, branch):
    member = idx[1]
    branch[...] = (cot[...].astype(F32) * drop[...]).astype(BF)
    xhat, _ = standard(tiles[...])
    normed = xhat.astype(BF)
    normed_ref[...] = normed
    x_ref[:, : 3 * C] = nt(normed, w[...]).astype(BF)
    x_ref[:, 3 * C :] = nt(branch[...], w_out[...]).astype(BF)
    x = x_ref[...].astype(F32)
    lane_head = head_of(lanes(D), 16) & 3
    p = rows(T)
    for out, count, rate, shift in ((near, 128, 4, 2), (mid, 32, 16, 4), (far, 8, 64, 6)):
        first = (4 * member) & (rate - 1)
        chosen = jnp.where((p & (rate - 1)) == first + lane_head, x, 0.0).astype(BF)
        n = max(count, 16)
        pick = jnp.where((lanes(T, n) >> shift) == rows(n, T), 1.0, 0.0).astype(BF)
        out[...] = nn(pick, chosen)[:count].astype(BF)


def local_stats_kernel(idx, lens, x_ref, st, vt, bias):
    place = idx[0]
    first = place * T
    q = x_ref[:, :C]
    k = x_ref[:, C : 2 * C]
    vt[...] = turned(x_ref[:, 2 * C : 3 * C])
    bias[...] = bias_of(slide(first + rows(T), lens), slide(first + lanes(T), lens))

    def step(c, carry):
        qc = q * lane_mask(c).astype(BF)
        w = jnp.exp2(nt(k, qc) * C1 + bias[...])
        top = pl.multiple_of(c * HD, 16)
        st[pl.ds(top, HD), :] = nn(vt[pl.ds(top, HD), :], w.astype(BF))
        st[pl.ds(pl.multiple_of(C + 8 * c, 8), 8), :] = jnp.broadcast_to(
            jnp.sum(w, 0, keepdims=True), (8, T)
        )
        return carry

    lax.fori_loop(0, 4, step, 0, unroll=True)


def near_stats_kernel(idx, lens, n0, n1, st, vt):
    place = idx[0]
    k = jnp.concatenate([n0[:, C : 2 * C], n1[:, C : 2 * C]], 0)
    vt[...] = turned(jnp.concatenate([n0[:, 2 * C : 3 * C], n1[:, 2 * C : 3 * C]], 0))
    q = n0[:128, :C]

    def step(c, carry):
        qc = q * lane_mask(c).astype(BF)
        bias = bias_of(
            slide(base_near(rows(T), place) + c, lens),
            slide(place * T + lanes(128) * 4 + c, lens),
        )
        w = jnp.exp2(nt(k, qc) * C1 + bias)
        top = pl.multiple_of(c * HD, 16)
        st[pl.ds(top, HD), :] = nn(vt[pl.ds(top, HD), :], w.astype(BF))
        st[pl.ds(pl.multiple_of(C + 8 * c, 8), 8), :] = jnp.broadcast_to(
            jnp.sum(w, 0, keepdims=True), (8, 128)
        )
        return carry

    lax.fori_loop(0, 4, step, 0, unroll=True)


def stacked(own, count):
    wide = own.astype(F32)
    parts = [wide * lane_mask(c) for c in range(4)]
    if count * 4 < 128:
        parts.append(jnp.zeros((128 - 4 * count, C), F32))
    return jnp.concatenate(parts, 0).astype(BF)


def wide_bias(base, count, rate, member, place, lens):
    shift = count.bit_length() - 1
    off = ((4 * member) & (rate - 1)) + (lanes(128) >> shift)
    q_pos = place * T + (lanes(128) & (count - 1)) * rate + off
    k_pos = base + off
    return bias_of(slide(k_pos, lens), slide(q_pos, lens))


def far_count(level):
    return (32, 16, base_mid) if level == 0 else (8, 64, base_far)


def half_pair(g0, g1, level, a, b):
    lo = 256 * level
    return jnp.concatenate([g0[lo : lo + 256, a:b], g1[lo : lo + 256, a:b]], 0)


def split3(x):
    hi = x.astype(BF).astype(F32)
    mid = (x - hi).astype(BF).astype(F32)
    lo = (x - hi - mid).astype(BF).astype(F32)
    return hi, mid, lo


def combine_kernel(idx, lens, x_ref, st_local, st_near, g0, g1, heads, heads_t, full, own, aux_n, aux_m, aux_f, acc):
    place, member = idx[0], idx[1]
    p = lanes(T)
    rh = row_head(C + 32)
    acc[...] = st_local[...] + spread(st_near[...], route_near(), (p & 3) == rh)
    for level in range(2):
        count, rate, base = far_count(level)
        shift = count.bit_length() - 1
        lo = 256 * level
        k = half_pair(g0, g1, level, C, 2 * C)
        vt = turned(half_pair(g0, g1, level, 2 * C, 3 * C))
        qbd = stacked(g0[lo : lo + max(count, 16), :C][:count], count)
        bias = wide_bias(base(rows(T), place), count, rate, member, place, lens)
        w = jnp.exp2(nt(k, qbd) * C1 + bias)
        lane_head = lanes(128) >> shift
        numer = nn(vt, w.astype(BF))
        totals = jnp.broadcast_to(jnp.sum(w, 0, keepdims=True), (32, 128))
        both = jnp.where(rh == lane_head, jnp.concatenate([numer, totals], 0), 0.0)
        route = route_mid() if level == 0 else route_far()
        ok = (p & (rate - 1)) == ((4 * member) & (rate - 1)) + rh
        acc[...] = acc[...] + spread(both, route, ok)
    gt = jnp.transpose(x_ref[:, 3 * C :].astype(F32))
    r8 = rows(8)
    pieces, mixes = [], []
    for c in range(4):
        total = acc[C + 8 * c : C + 8 * c + 1, :]
        mixed = acc[HD * c : HD * (c + 1), :] / total
        delta = jnp.sum(gt[HD * c : HD * (c + 1), :] * mixed, 0, keepdims=True)
        mixes.append(mixed)
        piece = jnp.zeros((8, T), F32)
        for j, part in enumerate(split3(jnp.log2(total)) + split3(delta)):
            piece = jnp.where(r8 == j, part, piece)
        pieces.append(piece)
    mixed = jnp.concatenate(mixes, 0)
    heads_t[...] = mixed.astype(BF)
    heads[...] = jnp.transpose(mixed).astype(BF)
    a32 = jnp.concatenate(pieces, 0)
    full[...] = a32
    rh32 = rows(32) >> 3
    for i, (rate, route, out, count) in enumerate(
        (
            (4, route_near(), aux_n, 128),
            (16, route_mid(), aux_m, 32),
            (64, route_far(), aux_f, 8),
        )
    ):
        ok = (p & (rate - 1)) == ((4 * member) & (rate - 1)) + rh32
        picked = nt(jnp.where(ok, a32, 0.0).astype(BF), route)
        own[32 * i : 32 * (i + 1), :] = picked
        square = jnp.concatenate([picked, jnp.zeros((96, 128), F32)], 0)
        out[...] = jnp.transpose(square)[:count].astype(BF)


def lse_of(a, c):
    return a[8 * c : 8 * c + 1] + a[8 * c + 1 : 8 * c + 2] + a[8 * c + 2 : 8 * c + 3]


def delta_of(a, c):
    return a[8 * c + 3 : 8 * c + 4] + a[8 * c + 4 : 8 * c + 5] + a[8 * c + 5 : 8 * c + 6]


def local_grads_kernel(idx, lens, x_ref, full, gqt, kv_ref, kt, bias, rowv):
    first = idx[0] * T
    q = x_ref[:, :C]
    k = x_ref[:, C : 2 * C]
    v = x_ref[:, 2 * C : 3 * C]
    g = x_ref[:, 3 * C :]
    kt[...] = turned(k)
    bias[...] = bias_of(slide(first + rows(T), lens), slide(first + lanes(T), lens))
    a = full[...]
    for c in range(4):
        rowv[c, 0:1, :] = lse_of(a, c)
        rowv[c, 1:2, :] = delta_of(a, c)
    kv_ref[...] = jnp.zeros((T, 2 * C), F32)

    def step(c, carry):
        m = lane_mask(c)
        mb = m.astype(BF)
        top = pl.multiple_of(c * HD, 16)
        w = jnp.exp2(nt(k, q * mb) * C1 + bias[...] - rowv[c, 0:1, :])
        low = w.astype(BF)
        ds = (w * (nt(v, g * mb) - rowv[c, 1:2, :])).astype(BF)
        kv_ref[:, :C] = kv_ref[:, :C] + nn(ds, q) * (m * FACTOR)
        kv_ref[:, C:] = kv_ref[:, C:] + nn(low, g) * m
        gqt[pl.ds(top, HD), :] = nn(kt[pl.ds(top, HD), :], ds)
        return carry

    lax.fori_loop(0, 4, step, 0, unroll=True)


def pack(keep_ref, send_ref, mine, parts):
    for j in range(8):
        block = mine ^ j
        out = keep_ref if j % 2 == 0 else send_ref
        lo = 96 * (j // 2)
        picked = [p[pl.ds(pl.multiple_of(block * n, 8), n), :] for p, n in parts]
        out[lo : lo + 96, :] = jnp.concatenate(picked, 0).astype(BF)


def query_grads_kernel(
    idx, lens, n0, n1, g0, g1, own, gqt, heads_t, branch, normed,
    gq_ref, term_q, term_out, kt, rowv, near_t,
):
    place, member = idx[0], idx[1]
    first = place * T
    o = own[...]
    for c in range(4):
        rowv[c, 2:3, 0:128] = lse_of(o[:32], c)
        rowv[c, 3:4, 0:128] = delta_of(o[:32], c)
    kn = jnp.concatenate([n0[:, C : 2 * C], n1[:, C : 2 * C]], 0)
    vn = jnp.concatenate([n0[:, 2 * C : 3 * C], n1[:, 2 * C : 3 * C]], 0)
    kt[...] = turned(kn)
    qn = n0[:128, :C]
    gn = n0[:128, 3 * C :]

    def near_step(c, carry):
        mb = lane_mask(c).astype(BF)
        top = pl.multiple_of(c * HD, 16)
        b = bias_of(
            slide(base_near(rows(T), place) + c, lens),
            slide(first + lanes(128) * 4 + c, lens),
        )
        w = jnp.exp2(nt(kn, qn * mb) * C1 + b - rowv[c, 2:3, 0:128])
        ds = (w * (nt(vn, gn * mb) - rowv[c, 3:4, 0:128])).astype(BF)
        near_t[pl.ds(top, HD), :] = nn(kt[pl.ds(top, HD), :], ds)
        return carry

    lax.fori_loop(0, 4, near_step, 0, unroll=True)
    p = lanes(T)
    rh = row_head(C)
    total = gqt[...] + spread(near_t[...], route_near(), (p & 3) == rh)
    for level in range(2):
        count, rate, base = far_count(level)
        shift = count.bit_length() - 1
        lo = 256 * level
        kk = half_pair(g0, g1, level, C, 2 * C)
        vv = half_pair(g0, g1, level, 2 * C, 3 * C)
        qbd = stacked(g0[lo : lo + max(count, 16), :C][:count], count)
        gbd = stacked(g0[lo : lo + max(count, 16), 3 * C :][:count], count)
        b = wide_bias(base(rows(T), place), count, rate, member, place, lens)
        lane_head = lanes(128) >> shift
        ol = o[32 + 32 * level : 64 + 32 * level]
        lse = jnp.zeros((1, 128), F32)
        delta = jnp.zeros((1, 128), F32)
        for c in range(4):
            lse = jnp.where(lane_head == c, lse_of(ol, c), lse)
            delta = jnp.where(lane_head == c, delta_of(ol, c), delta)
        w = jnp.where(lane_head < 4, jnp.exp2(nt(kk, qbd) * C1 + b - lse), 0.0)
        ds = (w * (nt(vv, gbd) - delta)).astype(BF)
        part = jnp.where(rh == lane_head, nn(turned(kk), ds), 0.0)
        route = route_mid() if level == 0 else route_far()
        ok = (p & (rate - 1)) == ((4 * member) & (rate - 1)) + rh
        total = total + spread(part, route, ok)
    total = total * FACTOR
    gq_ref[...] = jnp.transpose(total).astype(BF)
    term_out[...] = nn(heads_t[...], branch[...])
    term_q[...] = nn(total.astype(BF), normed[...])


def key_grads_kernel(
    idx, lens, n0, n1, g0, g1, a0, a1, kv, normed, term_q, term_out,
    gkv_ref, keep_ref, send_ref, rowv, sel, term,
):
    place, member = idx[0], idx[1]

    def aux_rows(level):
        lo = 256 * level
        both = jnp.concatenate([a0[lo : lo + 256, :], a1[lo : lo + 256, :]], 0)
        return jnp.transpose(both.astype(F32))

    near = aux_rows(0)
    for c in range(4):
        rowv[c, 0:1, :] = lse_of(near, c)
        rowv[c, 1:2, :] = delta_of(near, c)
    qn = jnp.concatenate([n0[:, :C], n1[:, :C]], 0)
    gn = jnp.concatenate([n0[:, 3 * C :], n1[:, 3 * C :]], 0)
    kn = n0[:128, C : 2 * C]
    vn = n0[:128, 2 * C : 3 * C]
    sel[...] = jnp.zeros((128, 2 * C), F32)

    def near_step(c, carry):
        m = lane_mask(c)
        mb = m.astype(BF)
        b = bias_of(
            slide(place * T + rows(128) * 4 + c, lens),
            slide(base_near(lanes(T), place) + c, lens),
        )
        w = jnp.exp2(nt(kn * mb, qn) * C1 + b - rowv[c, 0:1, :])
        low = w.astype(BF)
        ds = (w * (nt(vn * mb, gn) - rowv[c, 1:2, :])).astype(BF)
        sel[:, :C] = sel[:, :C] + nn(ds, qn) * m
        sel[:, C:] = sel[:, C:] + nn(low, gn) * m
        return carry

    lax.fori_loop(0, 4, near_step, 0, unroll=True)
    p = rows(T)
    lane_head8 = head_of(lanes(2 * C), 8) & 3
    scale = jnp.where(lanes(2 * C) < C, FACTOR, 1.0)

    def place_rows(x, rate, shift, count):
        take = jnp.where((rows(T, count) >> shift) == lanes(count, T), 1.0, 0.0).astype(BF)
        hi = x.astype(BF)
        lo = (x - hi.astype(F32)).astype(BF)
        ok = (p & (rate - 1)) == ((4 * member) & (rate - 1)) + lane_head8
        return jnp.where(ok, nn(take, hi) + nn(take, lo), 0.0)

    total = place_rows(sel[...], 4, 2, 128)
    for level in range(2):
        count, rate, base = far_count(level)
        shift = count.bit_length() - 1
        lo = 256 * level
        q = half_pair(g0, g1, level, 0, C)
        g = half_pair(g0, g1, level, 3 * C, 4 * C)
        kbd = stacked(g0[lo : lo + max(count, 16), C : 2 * C][:count], count)
        vbd = stacked(g0[lo : lo + max(count, 16), 2 * C : 3 * C][:count], count)
        row_c = rows(128) >> shift
        off = ((4 * member) & (rate - 1)) + row_c
        b = bias_of(
            slide(place * T + (rows(128) & (count - 1)) * rate + off, lens),
            slide(base(lanes(T), place) + off, lens),
        )
        aux = aux_rows(level + 1)
        lse = jnp.zeros((1, T), F32)
        delta = jnp.zeros((1, T), F32)
        for c in range(4):
            lse = jnp.where(row_c == c, lse_of(aux, c), lse)
            delta = jnp.where(row_c == c, delta_of(aux, c), delta)
        w = jnp.where(row_c < 4, jnp.exp2(nt(kbd, q) * C1 + b - lse), 0.0)
        ds = (w * (nt(vbd, g) - delta)).astype(BF)
        both = jnp.concatenate([nn(ds, q), nn(w.astype(BF), g)], 1)
        both = jnp.where(row_c == lane_head8, both, 0.0)
        merged = both[:count]
        for c in range(1, 4):
            merged = merged + both[c * count : (c + 1) * count]
        total = total + place_rows(
            jnp.concatenate([merged, jnp.zeros((128 - count, 2 * C), F32)], 0), rate, 4 if level == 0 else 6, 128
        )
    gkv = kv[...] + total * scale
    gkv_ref[...] = gkv.astype(BF)
    term[...] = nn(turned(gkv), normed[...])
    pack(keep_ref, send_ref, place & 7, ((term_q, 24), (term_out, 24), (term, 48)))


def back_kernel(idx, gq, gkv, w, b0, b1, b2, b3):
    for j, out in enumerate((b0, b1, b2, b3)):
        at = pl.ds(pl.multiple_of((idx[1] ^ j) * 128, 128), 128)
        out[...] = (nn(gq[at, :], w[:C, :]) + nn(gkv[at, :], w[C:, :])).astype(BF)


def layer_kernel(idx, salt, h0, h1, h2, h3, w0, w1, w2, w3, out):
    drop = jnp.where(keep(salt[0], idx[0] * T, T), DROP, 0.0)
    first = nn(h0[...], w0[...]) + nn(h1[...], w1[...])
    second = nn(h2[...], w2[...]) + nn(h3[...], w3[...])
    out[...] = ((first + second) * drop).astype(BF)


def tile_kernel(idx, tiles, b0, b1, b2, b3, out):
    at = pl.ds(pl.multiple_of(idx[1] * 128, 128), 128)
    xhat, inv = standard(tiles[at, :])
    g = b0[...].astype(F32) + b1[...].astype(F32) + b2[...].astype(F32) + b3[...].astype(F32)
    mean = jnp.mean(g, -1, keepdims=True)
    cross = jnp.mean(g * xhat, -1, keepdims=True)
    out[...] = (inv * (g - mean - xhat * cross)).astype(BF)


def join_kernel(idx, t0, t1, t2, t3, out, sems):
    copies = [
        pltpu.make_async_copy(
            t, out.at[pl.ds(pl.multiple_of((idx[1] ^ j) * 128, 128), 128), :], sems.at[j]
        )
        for j, t in enumerate((t0, t1, t2, t3))
    ]
    for copy in copies:
        copy.start()
    for copy in copies:
        copy.wait()


def finish_kernel(scale, idx, s0, s1, gw, go, wide, sems):
    mine = idx[0] & 7
    copies = []
    for j in range(8):
        block = mine ^ j
        lo = 96 * (j // 2)
        src = s0 if j % 2 == 0 else s1
        wide[j] = src[lo : lo + 96, :].astype(F32) * scale
        narrow = pl.ds(pl.multiple_of(block * 24, 8), 24)
        broad = pl.ds(pl.multiple_of(C + block * 48, 16), 48)
        for i, (part, dst) in enumerate(
            (
                (wide.at[j, 0:24, :], gw.at[narrow, :]),
                (wide.at[j, 24:48, :], go.at[narrow, :]),
                (wide.at[j, 48:96, :], gw.at[broad, :]),
            )
        ):
            copy = pltpu.make_async_copy(part, dst, sems.at[3 * j + i])
            copy.start()
            copies.append(copy)
    for copy in copies:
        copy.wait()


def call(kernel, n_scalar, args, outs, scratch=(), flops=0, sems=0):
    specs = [pl.BlockSpec(memory_space=pltpu.SMEM)] * n_scalar
    specs += [pl.BlockSpec(memory_space=pltpu.VMEM)] * (len(args) - n_scalar)
    return pl.pallas_call(
        kernel,
        in_specs=specs,
        out_specs=[pl.BlockSpec(memory_space=pltpu.HBM if sems else pltpu.VMEM)] * len(outs),
        out_shape=[jax.ShapeDtypeStruct(s, d) for s, d in outs],
        scratch_shapes=[pltpu.VMEM(s, d) for s, d in scratch]
        + ([pltpu.SemaphoreType.DMA((sems,))] if sems else []),
        compiler_params=pltpu.CompilerParams(vmem_limit_bytes=40 * 2**20),
        cost_estimate=pl.CostEstimate(flops=flops, bytes_accessed=flops // 200, transcendentals=0),
    )(*args)


def shards(tiles, w_qkv, w_out, slide_lengths, drop_salt, cotangent):
    member = lax.axis_index("mp")
    place = lax.axis_index("seq")
    groups = lax.axis_size("seq")
    idx = jnp.stack([place, member]).astype(I32)

    def swap(x, mask):
        return lax.ppermute(x, "seq", [(i, i ^ mask) for i in range(groups)])

    def along(i, bit):
        gray = (i >> 3) ^ (i >> 4) ^ bit
        return (gray ^ (gray >> 1) ^ (gray >> 2)) << 3 | i & 7

    def z_swap(x, bit):
        return lax.ppermute(x, "seq", [(i, along(i, bit)) for i in range(groups)])

    def across(x, mask):
        return lax.ppermute(x, "mp", [(i, i ^ mask) for i in range(4)])

    def tie(a, b):
        return lax.optimization_barrier((a, b))

    cat = jnp.concatenate
    us = 10**9
    w_t = w_qkv.T
    w_in = [across(w_out, j) for j in range(1, 4)]

    (drop,) = call(drop_kernel, 2, (idx, drop_salt), [((T, D), F32)], flops=3 * us)
    x, near, mid, far, normed, branch = call(
        start_kernel, 1, (idx, tiles, w_t, w_out, cotangent, drop),
        [((T, D), BF), ((128, D), BF), ((32, D), BF), ((8, D), BF), ((T, D), BF), ((T, D), BF)],
        flops=4 * us,
    )
    got = z_swap(far, 4)
    got_n = swap(near, 2)
    (st_local,) = call(
        local_stats_kernel, 2, (idx, slide_lengths, x),
        [((C + 32, T), F32)], [((C, T), BF), ((T, T), F32)], flops=5 * us,
    )
    (got, got_n), st_local = tie((got, got_n), st_local)
    far = cat([far, got], 0)
    n0 = cat([near, got_n], 0)
    n1 = swap(n0, 1)
    got, w_in = tie(z_swap(far, 2), w_in)
    far = cat([far, got], 0)
    got = swap(cat([mid, far], 0), 8)
    (st_near,) = call(
        near_stats_kernel, 2, (idx, slide_lengths, n0, n1),
        [((C + 32, 128), F32)], [((C, T), BF)], flops=2 * us,
    )
    got, st_near = tie(got, st_near)
    both = cat([mid, got[:32], far, got[32:]], 0)
    got = [both, swap(both, 2), swap(both, 4), swap(both, 6)]
    g0 = cat([b[:64] for b in got] + [b[64:] for b in got], 0)
    g1 = swap(g0, 1)

    heads, heads_t, full, own, aux_n, aux_m, aux_f = call(
        combine_kernel, 2, (idx, slide_lengths, x, st_local, st_near, g0, g1),
        [((T, C), BF), ((C, T), BF), ((32, T), F32), ((96, 128), F32), ((128, 128), BF), ((32, 128), BF), ((8, 128), BF)],
        [((C + 32, T), F32)], flops=4 * us,
    )
    def wide(a):
        return a.astype(F32)

    def cut(part):
        return [part[96 * i : 96 * (i + 1)] for i in range(4)]

    def x_swaps(pieces):
        return [swap(pieces[i], 2 * i) for i in range(1, 4)]

    def x_sum(pieces, got):
        return (wide(pieces[0]) + (wide(got[0]) + wide(got[1])) + wide(got[2])).astype(BF)

    def plus(part, got):
        return (wide(part) + wide(got)).astype(BF)

    got = z_swap(aux_f, 4)
    p_in = [across(heads, j) for j in range(1, 4)]
    gqt, kv = call(
        local_grads_kernel, 2, (idx, slide_lengths, x, full),
        [((C, T), F32), ((T, 2 * C), F32)],
        [((C, T), BF), ((T, T), F32), ((4, 8, T), F32)], flops=6 * us,
    )
    got, gqt = tie(got, gqt)
    far = cat([aux_f, got], 0)
    got = z_swap(far, 2)
    query = call(
        query_grads_kernel, 2,
        (idx, slide_lengths, n0, n1, g0, g1, own, gqt, heads_t, branch, normed),
        [((T, C), BF), ((C, D), F32), ((C, D), F32)],
        [((C, T), BF), ((4, 8, T), F32), ((C, 128), F32)], flops=6 * us,
    )
    got, ((gq, term_q, term_out), p_in) = tie(got, (query, p_in))
    far = cat([far, got], 0)
    got = swap(cat([aux_m, far], 0), 8)
    both = cat([aux_m, got[:32], far, got[32:]], 0)
    first, got = tie(swap(cat([both, aux_n], 0), 2), [swap(both, 4), swap(both, 6)])
    got = [both, first[:128]] + got
    a0 = cat([aux_n, first[128:]] + [b[:64] for b in got] + [b[64:] for b in got], 0)
    a1 = swap(a0, 1)

    key = call(
        key_grads_kernel, 2,
        (idx, slide_lengths, n0, n1, g0, g1, a0, a1, kv, normed, term_q, term_out),
        [((T, 2 * C), BF), ((384, D), BF), ((384, D), BF)],
        [((4, 8, T), F32), ((128, 2 * C), F32), ((2 * C, D), F32)], flops=5 * us,
    )
    gkv, kept, sent = key
    got = swap(sent, 1)
    back = call(back_kernel, 1, (idx, gq, gkv, w_t), [((128, D), BF)] * 4, flops=us)
    got, (b0, b1, b2, b3) = tie(got, back)
    part = cut(plus(kept, got))
    got = x_swaps(part)
    b_in = [across(b1, 1), across(b3, 3), across(b2, 2)]
    part = x_sum(part, got)
    got = swap(part, 8)
    (layer_out,) = call(
        layer_kernel, 2, (idx, drop_salt, heads, *p_in, w_out, *w_in), [((T, D), BF)], flops=2 * us
    )
    got, layer_out = tie(got, layer_out)
    part = plus(part, got)
    got = z_swap(part, 2)
    (t0,) = call(tile_kernel, 1, (idx, tiles, b0, *b_in), [((128, D), BF)], flops=us)
    got, t0 = tie(got, t0)
    part = plus(part, got)
    got = z_swap(part, 4)
    t_in = [across(t0, j) for j in range(1, 4)]
    part = plus(part, got)
    (tile_gradient,) = call(join_kernel, 1, (idx, t0, *t_in), [((T, D), BF)], flops=us, sems=4)
    got, tile_gradient = tie(x_swaps([part] * 4), tile_gradient)
    s0 = cat([part] + got, 0)
    s1 = swap(s0, 1)
    scale = (T * groups) ** -0.5

    def finish(*refs):
        finish_kernel(scale, *refs)

    grad_w_t, grad_w_out = call(
        finish, 1, (idx, s0, s1), [((3 * C, D), F32), ((C, D), F32)], [((8, 96, D), F32)], flops=us, sems=24
    )
    return (layer_out, tile_gradient, grad_w_t.T, grad_w_out)


def solution(mesh):
    placed = (P("seq", None), P(None, "mp"), P("mp", None), P(), P(), P("seq", None))
    return jax.shard_map(
        shards,
        mesh=mesh,
        in_specs=placed,
        out_specs=(P("seq", None), P("seq", None), P(None, "mp"), P("mp", None)),
        check_vma=False,
    )
```
